128 devices in a mesh: site: 8 (over x_hi, z), dom: 16 (over y, x_lo, core).
Axes of the slice: x: 4 (x_hi: 2, x_lo: 2; x = x_hi * 2 + x_lo), y: 4, z: 4, core: 2. Of those that a mesh axis runs over, the one named last changes fastest.
Arguments:
- fields: float32 [9, 128, 128, 256], P(None, 'dom', 'site'), may hold values from -6 to 6
- material: float32 [3, 128, 128, 256], P(None, 'dom', 'site'), may hold values from 0.3 to 1
- send_cell: int32 [8, 16, 16, 128], P('site', 'dom'), may hold values from -1 to 32767, as said below
- recv_node: int32 [8, 16, 16, 128], P('site', 'dom'), may hold values from -1 to 4095, as said below
- elements: int32 [8, 16, 8, 2048], P('site', 'dom'), may hold values from -1 to 4095, as said below
- modulus: float32 [8, 16, 2048], P('site', 'dom'), may hold values from 0.1 to 1
- node_mass: float32 [8, 16, 4096], P('site', 'dom'), may hold values from 0.5 to 2
- outer_flag: int32 [8, 16, 4096], P('site', 'dom'), may hold values 0 or 1
- shared_slot: int32 [8, 16, 4096], P('site', 'dom'), may hold values from -1 to 511, as said below
- stiffness: float32 [24, 24], replicated, as said below
- disp_now: float32 [8, 16, 3, 4096], P('site', 'dom'), may hold values from -0.1 to 0.1
- disp_prev: float32 [8, 16, 3, 4096], P('site', 'dom'), may hold values from -0.1 to 0.1
Outputs:
- basin_out: float32 [9, 128, 128, 256], P(None, 'dom', 'site')
- site_disp: float32 [8, 16, 3, 4096], P('site', 'dom')
The draws below stay inside these ranges and needn't reach their ends.
Inputs may be any that keep to these rules, and one draw needn't show every extreme that they name: `send_cell`: entry [s, p, q, c] is a cell of slab (s, p), to send to partition q of site model s, or -1. It is live exactly where recv_node[s, q, p, c] is live; live entries come first along c. For each site model the sending slabs are a run of max(half of 16, 1) consecutive slab indices (wrapping); each of their pairs has between half of 128 and 128 live entries, and the first slab of the run fills all 128 to every partition. `recv_node`: entry [s, q, p, c] is the node of partition q of site model s that takes slot c from slab (s, p), or -1; the live nodes of one partition are distinct. `elements`: columns are element slots; a padding slot has -1 in all eight rows and padding slots come last. Each partition has between half of 2048 and 2048 live slots, and in every site model one partition has all 2048. Live entries name nodes of the partition. `shared_slot`: each slot 0 to 511 names exactly one node of a partition; slots below 256 are shared with the previous partition of the site model, the others with the next one (wrapping); other nodes hold -1. `stiffness`: Symmetric.
All inputs are finite; a program needn't handle non-finite values. No bound on the sum of `outer_flag` on one device may be relied on, other than what follows from the above.
Results may differ from the reference program's by a relative error of at most 0.0003.
Values sent between devices are 32-bit elements; how exact they have to be, the bound alone decides.
A program may use at most 128 MiB of HBM per device.

```python
import math
import jax
import jax.numpy as jnp
from jax import lax

CX = 8
CY = 16
NZ = 256
STEPS = 3
NODES_DEV = 4096
ELEM_DEV = 2048
CAP = 128
SHARE = 256
SITES = 8
SECTIONS = 16
NX = 128
NY = 128


def drm_counts(key):
    key_start, key_count = jax.random.split(jax.random.fold_in(key, 7))
    start = jax.random.randint(key_start, (SITES,), 0, SECTIONS)
    width = max(SECTIONS // 2, 1)
    source = jnp.arange(SECTIONS, dtype=jnp.int32)
    offset = (source[None, :] - start[:, None]) % SECTIONS
    counts = jax.random.randint(key_count, (SITES, SECTIONS, SECTIONS), CAP // 2, CAP + 1)
    counts = jnp.where(offset[:, :, None] == 0, CAP, counts)
    return jnp.where((offset < width)[:, :, None], counts, 0)


def draw_send_cell(key, part):
    counts = drm_counts(key)
    cells = jax.random.randint(jax.random.fold_in(key, 13), (SITES, SECTIONS, SECTIONS, CAP), 0, CX * CY * NZ)
    live = jnp.arange(CAP, dtype=jnp.int32)[None, None, None, :] < counts[..., None]
    return jnp.where(live, cells, -1).astype(jnp.int32)


def draw_recv_node(key, part):
    counts = drm_counts(key)
    keys = jax.random.split(jax.random.fold_in(key, 11), SITES * SECTIONS)
    orders = jax.vmap(lambda one_key: jax.random.permutation(one_key, NODES_DEV)[:SECTIONS * CAP])(keys)
    orders = orders.reshape(SITES, SECTIONS, SECTIONS, CAP)
    live = jnp.arange(CAP, dtype=jnp.int32)[None, None, None, :] < jnp.transpose(counts, (0, 2, 1))[..., None]
    return jnp.where(live, orders, -1).astype(jnp.int32)


def draw_elements(key, part):
    key_nodes, key_count, key_full = jax.random.split(jax.random.fold_in(key, 23), 3)
    nodes = jax.random.randint(key_nodes, (SITES, SECTIONS, 8, ELEM_DEV), 0, NODES_DEV)
    counts = jax.random.randint(key_count, (SITES, SECTIONS), ELEM_DEV // 2, ELEM_DEV + 1)
    full = jax.random.randint(key_full, (SITES,), 0, SECTIONS)
    counts = jnp.where(jnp.arange(SECTIONS, dtype=jnp.int32)[None, :] == full[:, None], ELEM_DEV, counts)
    live = jnp.arange(ELEM_DEV, dtype=jnp.int32)[None, None, None, :] < counts[:, :, None, None]
    return jnp.where(live, nodes, -1).astype(jnp.int32)


def draw_shared_slot(key, part):
    keys = jax.random.split(jax.random.fold_in(key, 31), SITES * SECTIONS)
    orders = jax.vmap(lambda one_key: jnp.argsort(jax.random.permutation(one_key, NODES_DEV)))(keys)
    slots = jnp.where(orders < 2 * SHARE, orders, -1)
    return slots.reshape(SITES, SECTIONS, NODES_DEV).astype(jnp.int32)


def draw_stiffness(key, part):
    key_off, key_diag = jax.random.split(jax.random.fold_in(key, 41))
    raw = jax.random.uniform(key_off, (24, 24), jnp.float32, -1.0, 1.0)
    off_diag = 0.25 * (raw + raw.T)
    diag_vals = 1.0 + 0.5 * jax.random.uniform(key_diag, (24,), jnp.float32)
    eye_mask = jnp.eye(24, dtype=jnp.float32) > 0.5
    return jnp.where(eye_mask, diag_vals[:, None] * jnp.ones((24, 24), jnp.float32), off_diag).astype(jnp.float32)


def with_ends(array, key, low, largest):
    dims = array.shape
    spot = [jax.random.randint(jax.random.fold_in(key, axis), (), 0, dims[axis]) for axis in range(len(dims))]
    array = array.at[tuple(spot)].set(low)
    longest = dims.index(max(dims))
    spot[longest] = (spot[longest] + 1) % dims[longest]
    return array.at[tuple(spot)].set(largest)


def block_levels(own_key, extent, pieces, smallest, high):
    gain, own = 1.0, jax.random.fold_in(own_key, 6)
    for axis_at, blocks in pieces:
        heights = jnp.exp(jax.random.uniform(jax.random.fold_in(own, axis_at), (blocks,), jnp.float32, smallest / len(pieces), high / len(pieces)))
        gain = gain * jnp.repeat(heights, extent[axis_at] // blocks).reshape([-1 if axis == axis_at else 1 for axis in range(len(extent))])
    return gain


def normal_values(rng, dims, deviation, reach, cuts=(), kind=jnp.bfloat16):
    gain = block_levels(rng, dims, cuts, -0.22, 0.18) if cuts else 1.0
    drawn = jax.random.normal(rng, dims, jnp.float32) * deviation * gain
    return jnp.minimum(jnp.maximum(drawn, -reach), reach).astype(kind)


def setup_inputs(seed: int = 0) -> dict:
    key_of = jax.random.split(jax.random.key(seed), 13)
    return {
        "fields": normal_values(key_of[0], (9, NX, NY, NZ), 1.0, 6.0, ((1, 16), (2, 8)), jnp.float32),
        "material": jnp.clip(jnp.exp(math.log(1.0) - 1.2039728 * jax.random.uniform(key_of[1], (3, NX, NY, NZ), jnp.float32) ** block_levels(key_of[1], (3, NX, NY, NZ), ((1, 16), (2, 8)), -0.2, 0.2)), 0.3, 1.0),
        "send_cell": draw_send_cell(jax.random.fold_in(key_of[12], 71), 0),
        "recv_node": draw_recv_node(jax.random.fold_in(key_of[12], 71), 0),
        "elements": draw_elements(jax.random.fold_in(key_of[12], 71), 0),
        "modulus": jnp.clip(jnp.exp(math.log(1.0) - 2.3025851 * jax.random.uniform(key_of[5], (SITES, SECTIONS, ELEM_DEV), jnp.float32) ** block_levels(key_of[5], (SITES, SECTIONS, ELEM_DEV), ((0, 8), (1, 16)), -0.2, 0.2)), 0.1, 1.0),
        "node_mass": jnp.clip(jnp.exp(math.log(2.0) - 1.3862944 * jax.random.uniform(key_of[6], (SITES, SECTIONS, NODES_DEV), jnp.float32) ** block_levels(key_of[6], (SITES, SECTIONS, NODES_DEV), ((0, 8), (1, 16)), -0.2, 0.2)), 0.5, 2.0),
        "outer_flag": with_ends((jax.random.randint(key_of[7], (SITES, SECTIONS, NODES_DEV), 0, 2) < 1).astype(jnp.int32), jax.random.fold_in(key_of[7], 1), 0, 1),
        "shared_slot": draw_shared_slot(jax.random.fold_in(key_of[12], 71), 0),
        "stiffness": draw_stiffness(jax.random.fold_in(key_of[12], 71), 0),
        "disp_now": jnp.clip(jax.random.uniform(key_of[10], (SITES, SECTIONS, 3, NODES_DEV), jnp.float32, -0.1, 0.1) * block_levels(key_of[10], (SITES, SECTIONS, 3, NODES_DEV), ((0, 8), (1, 16)), -0.4, 0.0), -0.1, 0.1),
        "disp_prev": jnp.clip(jax.random.uniform(key_of[11], (SITES, SECTIONS, 3, NODES_DEV), jnp.float32, -0.1, 0.1) * block_levels(key_of[11], (SITES, SECTIONS, 3, NODES_DEV), ((0, 8), (1, 16)), -0.4, 0.0), -0.1, 0.1),
    }


C_NEAR = 9.0 / 8.0
C_FAR = 1.0 / 24.0
DT_BASIN = 0.25
DT_SITE2 = 0.15


def forward_diff(padded, along, length):
    def window(offset):
        return lax.slice_in_dim(padded, offset, offset + length, axis=along)
    return C_NEAR * (window(3) - window(2)) - C_FAR * (window(4) - window(1))


def backward_diff(padded, along, length):
    def window(offset):
        return lax.slice_in_dim(padded, offset, offset + length, axis=along)
    return C_NEAR * (window(2) - window(1)) - C_FAR * (window(3) - window(0))


def pad_along(field, along):
    widths = [(0, 0)] * field.ndim
    widths[along] = (2, 2)
    return jnp.pad(field, widths)


def fwd(field, along):
    return forward_diff(pad_along(field, along), along, field.shape[along])


def bwd(field, along):
    return backward_diff(pad_along(field, along), along, field.shape[along])


def basin_step(velocity, stress, material):
    buoyancy = material[0]
    vel_x = velocity[0] + DT_BASIN * buoyancy * (fwd(stress[0], 0) + bwd(stress[3], 1) + bwd(stress[4], 2))
    vel_y = velocity[1] + DT_BASIN * buoyancy * (bwd(stress[3], 0) + fwd(stress[1], 1) + bwd(stress[5], 2))
    vel_z = velocity[2] + DT_BASIN * buoyancy * (bwd(stress[4], 0) + bwd(stress[5], 1) + fwd(stress[2], 2))
    lame_first, shear_mod = material[1], material[2]
    strain_xx = bwd(vel_x, 0)
    strain_yy = bwd(vel_y, 1)
    strain_zz = bwd(vel_z, 2)
    modulus_p = lame_first + 2.0 * shear_mod
    new_xx = stress[0] + DT_BASIN * (modulus_p * strain_xx + lame_first * (strain_yy + strain_zz))
    new_yy = stress[1] + DT_BASIN * (modulus_p * strain_yy + lame_first * (strain_xx + strain_zz))
    new_zz = stress[2] + DT_BASIN * (modulus_p * strain_zz + lame_first * (strain_xx + strain_yy))
    new_xy = stress[3] + DT_BASIN * shear_mod * (fwd(vel_x, 1) + fwd(vel_y, 0))
    new_xz = stress[4] + DT_BASIN * shear_mod * (fwd(vel_x, 2) + fwd(vel_z, 0))
    new_yz = stress[5] + DT_BASIN * shear_mod * (fwd(vel_y, 2) + fwd(vel_z, 1))
    return jnp.stack([vel_x, vel_y, vel_z]), jnp.stack([new_xx, new_yy, new_zz, new_xy, new_xz, new_yz])


def sample_global(velocity, send_cell):
    safe = jnp.maximum(send_cell, 0)
    cell_x = safe // (CY * NZ)
    cell_y = (safe // NZ) % CY
    cell_z = safe % NZ
    global_x = jnp.arange(SECTIONS, dtype=jnp.int32)[None, :, None, None] * CX + cell_x
    global_y = jnp.arange(SITES, dtype=jnp.int32)[:, None, None, None] * CY + cell_y
    values = velocity[:, global_x, global_y, cell_z]
    return jnp.where(send_cell[None] >= 0, values, 0.0)


def place_motion(values, nodes):
    target = jnp.where(nodes >= 0, nodes, NODES_DEV).reshape(-1)
    return jnp.zeros((3, NODES_DEV), jnp.float32).at[:, target].set(values.reshape(3, -1), mode="drop")


def drm_nodes(nodes):
    target = jnp.where(nodes >= 0, nodes, NODES_DEV).reshape(-1)
    return jnp.zeros((NODES_DEV,), jnp.float32).at[target].set(1.0, mode="drop")


def slot_nodes(slots):
    target = jnp.where(slots >= 0, slots, 2 * SHARE)
    return jnp.zeros((2 * SHARE,), jnp.int32).at[target].set(jnp.arange(NODES_DEV, dtype=jnp.int32), mode="drop")


def site_forces(displacement, free_field, drm_mask, outer, element_nodes, element_mod, stiffness):
    count = element_nodes.shape[1]
    live = (element_nodes[0] >= 0).astype(jnp.float32)
    safe = jnp.maximum(element_nodes, 0)
    mask_outer = drm_mask * outer
    mask_inner = drm_mask * (1.0 - outer)
    stacked = jnp.stack([displacement, free_field * mask_inner, free_field * mask_outer])
    gathered = stacked[:, :, safe].reshape(3, 24, count)
    gathered = jnp.transpose(gathered, (1, 0, 2)).reshape(24, 3 * count)
    response = jnp.dot(stiffness, gathered, precision=lax.Precision.HIGHEST,
                       preferred_element_type=jnp.float32).reshape(24, 3, count)
    outer_rows = jnp.tile(mask_outer[safe], (3, 1))
    inner_rows = jnp.tile(mask_inner[safe], (3, 1))
    force = (element_mod * live) * (-response[:, 0] + outer_rows * response[:, 1] - inner_rows * response[:, 2])
    return jnp.zeros((3, NODES_DEV), jnp.float32).at[:, safe.reshape(-1)].add(force.reshape(3, 8 * count))


def set_slots(force, nodes, total):
    return force.at[:, nodes].set(total)


def reference(fields, material, send_cell, recv_node, elements, modulus, node_mass, outer_flag, shared_slot, stiffness, disp_now, disp_prev):
    velocity, stress = fields[0:3], fields[3:9]
    samples = []
    for segment in range(STEPS):
        velocity, stress = basin_step(velocity, stress, material)
        samples.append(sample_global(velocity, send_cell))
    basin_out = jnp.concatenate([velocity, stress], axis=0)
    place_all = jax.vmap(jax.vmap(place_motion))
    drm_mask = jax.vmap(jax.vmap(drm_nodes))(recv_node)
    slot_node = jax.vmap(jax.vmap(slot_nodes))(shared_slot)
    outer = outer_flag.astype(jnp.float32)
    forces_all = jax.vmap(jax.vmap(site_forces, in_axes=(0, 0, 0, 0, 0, 0, None)), in_axes=(0, 0, 0, 0, 0, 0, None))
    set_all = jax.vmap(jax.vmap(set_slots))
    displacement, previous = disp_now, disp_prev
    free_field = jnp.zeros_like(disp_now)
    for segment in range(STEPS):
        arrived = jnp.transpose(samples[segment], (1, 3, 0, 2, 4))
        free_field = free_field + DT_BASIN * place_all(arrived, recv_node)
        force = forces_all(displacement, free_field, drm_mask, outer, elements, modulus, stiffness)
        partial_sum = jnp.take_along_axis(force, slot_node[:, :, None, :], axis=3)
        left_side = jnp.roll(partial_sum, 1, axis=1)
        right_side = jnp.roll(partial_sum, -1, axis=1)
        total = jnp.concatenate([partial_sum[..., :SHARE] + left_side[..., SHARE:],
                                 partial_sum[..., SHARE:] + right_side[..., :SHARE]], axis=3)
        force = set_all(force, slot_node, total)
        following = (2.0 * displacement - previous) + DT_SITE2 * force / node_mass[:, :, None, :]
        previous, displacement = displacement, following
    return basin_out, displacement
```

```python
import functools

import jax
import jax.numpy as jnp
from jax import lax
from jax.experimental import pallas as pl
from jax.experimental.pallas import tpu as pltpu
from jax.sharding import PartitionSpec as P

STEPS = 3
SHARE = 256
C_NEAR = 9.0 / 8.0
C_FAR = 1.0 / 24.0
DT = 0.25
DT_SITE2 = 0.15
MESH = pl.DeviceIdType.MESH
LANES = 128
COLS = 256
F32 = jnp.float32
BF16 = jnp.bfloat16
NT = (((1,), (1,)), ((), ()))

STRESS_X = ((3, "F"), (6, "B"), (7, "B"))
STRESS_Y = ((6, "B"), (4, "F"), (8, "B"))
VEL_X = ((0, "B"), (1, "F"), (2, "F"))
VEL_Y = ((0, "F"), (1, "B"), (2, "F"))
LOW = {"B": 2, "F": 1}
HIGH = {"B": 1, "F": 2}


def take_lanes(table, lanes):
    return lax.gather(
        table,
        lanes[..., None],
        lax.GatherDimensionNumbers(
            offset_dims=(),
            collapsed_slice_dims=(1,),
            start_index_map=(1,),
            operand_batching_dims=(0,),
            start_indices_batching_dims=(0,),
        ),
        (1, 1),
        mode=lax.GatherScatterMode.PROMISE_IN_BOUNDS,
    )


def stencil(kind, m2, m1, f, p1, p2):
    if kind == "B":
        return C_NEAR * (f - m1) - C_FAR * (p1 - m2)
    return C_NEAR * (p1 - f) - C_FAR * (p2 - m1)


def diff_rolled(kind, f, axis, index, low, high):
    n = f.shape[axis]
    below = lambda v, edge: jnp.where(index == 0, edge, pltpu.roll(v, 1, axis))
    above = lambda v, edge: jnp.where(index == n - 1, edge, pltpu.roll(v, n - 1, axis))
    m1 = below(f, low[-1])
    p1 = above(f, high[0])
    if kind == "B":
        return stencil(kind, below(m1, low[0]), m1, f, p1, None)
    return stencil(kind, None, m1, f, p1, above(p1, high[1]))


def split(v):
    top = v.astype(BF16).astype(F32)
    return top, v - top


def kernel(
    n_site,
    n_dom,
    fields,
    mat,
    send_cell,
    recv_node,
    elem,
    modulus,
    mass_in,
    flag_in,
    slot_in,
    stiff,
    now_in,
    prev_in,
    basin_out,
    disp_out,
    st,
    y_low,
    y_high,
    y_to_low,
    y_to_high,
    samp_send,
    samp_recv,
    rim_send,
    rim_recv,
    oh_recv,
    oh_elem,
    lhs,
    table,
    inn,
    out,
    cols,
    kblock,
    fe,
    u_now,
    u_prev,
    free,
    code,
    mass,
    slot,
    slot_node,
    force,
    in_sem,
    out_sem,
    x_send_sem,
    x_recv_sem,
    y_send_sem,
    y_recv_sem,
    s_send_sem,
    s_recv_sem,
    r_send_sem,
    r_recv_sem,
):
    cx, cy, nz = mat.shape[1:]
    rows_n = u_now.shape[1]
    n_el = elem.shape[1]
    n_arr = n_dom * LANES
    me_s = lax.axis_index("site")
    me_d = lax.axis_index("dom")

    load = pltpu.make_async_copy(fields, st.at[:, pl.ds(2, cx)], in_sem)
    load.start()
    st[:, pl.ds(0, 2)] = jnp.zeros((9, 2, cy, nz), F32)
    st[:, pl.ds(2 + cx, 2)] = jnp.zeros((9, 2, cy, nz), F32)
    y_low[...] = jnp.zeros(y_low.shape, F32)
    y_high[...] = jnp.zeros(y_high.shape, F32)

    barrier = pltpu.get_barrier_semaphore()

    def greet(d, carry):
        pl.semaphore_signal(
            barrier, inc=1, device_id=(me_s, lax.rem(me_d + d, n_dom)), device_id_type=MESH
        )
        return carry

    lax.fori_loop(1, n_dom, greet, 0)
    for step in (-1, 1):
        there = me_s + step

        @pl.when((there >= 0) & (there < n_site))
        def _():
            pl.semaphore_signal(barrier, inc=1, device_id=(there, me_d), device_id_type=MESH)

    load.wait()

    row_iota = lax.broadcasted_iota(jnp.int32, (cy, nz), 0)
    lane_iota = lax.broadcasted_iota(jnp.int32, (cy, nz), 1)

    def x_copies(which, fields_x, upward):
        made = []
        for at, (f, kind) in enumerate(fields_x):
            if upward:
                width = LOW[kind]
                src = st.at[f, pl.ds(2 + cx - width, width)]
                dst = st.at[f, pl.ds(2 - width, width)]
                there = me_d + 1
            else:
                width = HIGH[kind]
                src = st.at[f, pl.ds(2, width)]
                dst = st.at[f, pl.ds(2 + cx, width)]
                there = me_d - 1
            sem = (which, 1 if upward else 0, at)
            made.append(
                pltpu.make_async_remote_copy(
                    src_ref=src,
                    dst_ref=dst,
                    send_sem=x_send_sem.at[sem],
                    recv_sem=x_recv_sem.at[sem],
                    device_id=(me_s, there),
                    device_id_type=MESH,
                )
            )
        return made

    def y_copy(which, fields_y, upward):
        count = sum((LOW if upward else HIGH)[kind] for _, kind in fields_y)
        src, dst = (y_to_high, y_low) if upward else (y_to_low, y_high)
        sem = (which, 1 if upward else 0)
        return pltpu.make_async_remote_copy(
            src_ref=src.at[which, pl.ds(0, count)],
            dst_ref=dst.at[which, pl.ds(0, count)],
            send_sem=y_send_sem.at[sem],
            recv_sem=y_recv_sem.at[sem],
            device_id=(me_s + (1 if upward else -1), me_d),
            device_id_type=MESH,
        )

    has = {
        "x": (me_d > 0, me_d < n_dom - 1),
        "y": (me_s > 0, me_s < n_site - 1),
    }

    def halo_start(which, fields_x, fields_y):
        for upward in (False, True):

            @pl.when(has["x"][upward])
            def _():
                for copy in x_copies(which, fields_x, upward):
                    copy.start()

            @pl.when(has["y"][upward])
            def _():
                y_copy(which, fields_y, upward).start()

    def halo_wait(which, fields_x, fields_y):
        for upward in (False, True):

            @pl.when(has["x"][upward])
            def _():
                for copy in x_copies(which, fields_x, upward):
                    copy.wait_send()

            @pl.when(has["x"][not upward])
            def _():
                for copy in x_copies(which, fields_x, upward):
                    copy.wait_recv()

            @pl.when(has["y"][upward])
            def _():
                y_copy(which, fields_y, upward).wait_send()

            @pl.when(has["y"][not upward])
            def _():
                y_copy(which, fields_y, upward).wait_recv()

    def y_pack(which, fields_y, x, planes):
        at = 0
        for f, kind in fields_y:
            for k in range(LOW[kind]):
                y = cy - LOW[kind] + k
                y_to_high[which, at, pl.ds(x, 1), :] = planes[f][y : y + 1]
                at += 1
        at = 0
        for f, kind in fields_y:
            for k in range(HIGH[kind]):
                y_to_low[which, at, pl.ds(x, 1), :] = planes[f][k : k + 1]
                at += 1

    def y_edges(which, fields_y, x):
        edges = {}
        low_at = high_at = 0
        for f, kind in fields_y:
            low = [y_low[which, low_at + k, pl.ds(x, 1), :] for k in range(LOW[kind])]
            high = [y_high[which, high_at + k, pl.ds(x, 1), :] for k in range(HIGH[kind])]
            low_at += LOW[kind]
            high_at += HIGH[kind]
            edges[f] = (low, high)
        return edges

    def diff_x(kind, f, x):
        at = lambda o: st[f, x + 2 + o]
        if kind == "B":
            return stencil(kind, at(-2), at(-1), at(0), at(1), None)
        return stencil(kind, None, at(-1), at(0), at(1), at(2))

    def diff_y(kind, f, x, edges):
        low, high = edges[f]
        return diff_rolled(kind, st[f, x + 2], 0, row_iota, low, high)

    def diff_z(kind, f, x):
        return diff_rolled(kind, st[f, x + 2], 1, lane_iota, (0.0, 0.0), (0.0, 0.0))

    def velocity_half():
        def body(x, carry):
            edges = y_edges(0, STRESS_Y, x)
            b = DT * mat[0, x]
            planes = {
                0: st[0, x + 2]
                + b * (diff_x("F", 3, x) + diff_y("B", 6, x, edges) + diff_z("B", 7, x)),
                1: st[1, x + 2]
                + b * (diff_x("B", 6, x) + diff_y("F", 4, x, edges) + diff_z("B", 8, x)),
                2: st[2, x + 2]
                + b * (diff_x("B", 7, x) + diff_y("B", 8, x, edges) + diff_z("F", 5, x)),
            }
            for f, plane in planes.items():
                st[f, x + 2] = plane
            y_pack(1, VEL_Y, x, planes)
            return carry

        lax.fori_loop(0, cx, body, 0)

    def stress_half():
        def body(x, carry):
            edges = y_edges(1, VEL_Y, x)
            lam, mu = mat[1, x], mat[2, x]
            exx = diff_x("B", 0, x)
            eyy = diff_y("B", 1, x, edges)
            ezz = diff_z("B", 2, x)
            wide = lam + 2.0 * mu
            shear = DT * mu
            planes = {
                3: st[3, x + 2] + DT * (wide * exx + lam * (eyy + ezz)),
                4: st[4, x + 2] + DT * (wide * eyy + lam * (exx + ezz)),
                5: st[5, x + 2] + DT * (wide * ezz + lam * (exx + eyy)),
                6: st[6, x + 2] + shear * (diff_y("F", 0, x, edges) + diff_x("F", 1, x)),
                7: st[7, x + 2] + shear * (diff_z("F", 0, x) + diff_x("F", 2, x)),
                8: st[8, x + 2] + shear * (diff_z("F", 1, x) + diff_y("F", 2, x, edges)),
            }
            for f, plane in planes.items():
                st[f, x + 2] = plane
            y_pack(0, STRESS_Y, x, planes)
            return carry

        lax.fori_loop(0, cx, body, 0)

    def sample(k):
        cell = send_cell[...]
        low, high = cell & (LANES - 1), cell >> 7
        halves = nz // LANES

        def body(x, acc):
            acc = list(acc)
            for y in range(cy):
                for half in range(halves):
                    here = high == (x * cy + y) * halves + half
                    for c in range(3):
                        row = st[c, x + 2, y : y + 1, half * LANES : (half + 1) * LANES]
                        got = take_lanes(jnp.broadcast_to(row, cell.shape), low)
                        acc[c] = jnp.where(here, got, acc[c])
            return tuple(acc)

        acc = lax.fori_loop(0, cx, body, (jnp.zeros(cell.shape, F32),) * 3)
        for c in range(3):
            for q in range(n_dom):
                samp_send[k, q, c : c + 1, :] = acc[c][q : q + 1]

    def sample_copy(k, d):
        there = lax.rem(me_d + d, n_dom)
        return pltpu.make_async_remote_copy(
            src_ref=samp_send.at[k, there],
            dst_ref=samp_recv.at[k, me_d],
            send_sem=s_send_sem.at[k, d],
            recv_sem=s_recv_sem.at[k, d],
            device_id=(me_s, there),
            device_id_type=MESH,
        )

    def sample_start(k):
        def body(d, carry):
            sample_copy(k, d).start()
            return carry

        lax.fori_loop(1, n_dom, body, 0)
        samp_recv[k, me_d] = samp_send[k, me_d]

    def sample_wait(k):
        def body(d, carry):
            here = lax.rem(me_d + n_dom - d, n_dom)
            copy = pltpu.make_async_remote_copy(
                src_ref=samp_send.at[k, here],
                dst_ref=samp_recv.at[k, here],
                send_sem=s_send_sem.at[k, d],
                recv_sem=s_recv_sem.at[k, d],
                device_id=(me_s, here),
                device_id_type=MESH,
            )
            copy.wait_recv()
            sample_copy(k, d).wait_send()
            return carry

        lax.fori_loop(1, n_dom, body, 0)

    high_iota = lax.broadcasted_iota(jnp.int32, (rows_n, LANES), 0)

    def build_table(values, group):
        for h in range(rows_n):
            for half in range(COLS // LANES):
                row = values[h : h + 1, half * LANES : (half + 1) * LANES]
                table[group, h * (COLS // LANES) + half] = jnp.broadcast_to(row, (8, LANES))

    def look_up(index, groups):
        low, high = index & (LANES - 1), index >> 7
        acc = [jnp.zeros(index.shape, F32) for _ in groups]
        for r in range(rows_n * (COLS // LANES)):
            here = high == r
            for at, group in enumerate(groups):
                acc[at] = jnp.where(here, take_lanes(table[group, r], low), acc[at])
        return acc

    def one_hot_rows(low):
        iota = lax.broadcasted_iota(jnp.int32, (COLS, low.shape[1]), 0)
        return jnp.where(iota == low, 1.0, 0.0).astype(BF16)

    def site_prep():
        for h in range(rows_n):
            at = pl.ds(h * COLS, COLS)
            mass[h : h + 1] = mass_in[:, at]
            slot[h : h + 1] = slot_in[:, at]
            for c in range(3):
                u_now[c, h : h + 1] = now_in[c : c + 1, at]
                u_prev[c, h : h + 1] = prev_in[c : c + 1, at]
        free[...] = jnp.zeros(free.shape, F32)

        n_k = stiff.shape[0]
        n_r, n_c = kblock.shape
        ri = lax.broadcasted_iota(jnp.int32, (n_r, n_k), 0)
        rk = lax.broadcasted_iota(jnp.int32, (n_r, n_k), 1)
        pick_r = jnp.where(ri % n_k == rk, 1.0, 0.0)
        ck = lax.broadcasted_iota(jnp.int32, (n_k, n_c), 0)
        ci = lax.broadcasted_iota(jnp.int32, (n_k, n_c), 1)
        pick_c = jnp.where(ci % n_k == ck, 1.0, 0.0)
        exact = functools.partial(
            jnp.dot, precision=lax.Precision.HIGHEST, preferred_element_type=F32
        )
        tiled = exact(exact(pick_r, stiff[...]), pick_c)
        top, rest = split(tiled)
        rr = lax.broadcasted_iota(jnp.int32, (n_r, n_c), 0)
        cc = lax.broadcasted_iota(jnp.int32, (n_r, n_c), 1)
        part = (cc // n_k) % 3
        value = jnp.where(part == 2, rest, top)
        kblock[...] = jnp.where(rr // n_k == cc // (3 * n_k), value, 0.0).astype(BF16)

        def arrivals(p, carry):
            at = pl.ds(pl.multiple_of(p * LANES, LANES), LANES)
            node = recv_node[pl.ds(p, 1), :]
            oh_recv[:, at] = one_hot_rows(node & (COLS - 1))
            lhs[pl.ds(0, rows_n), at] = jnp.where((node >> 8) == high_iota, 1.0, 0.0).astype(BF16)
            return carry

        lax.fori_loop(0, n_dom, arrivals, 0)
        drm = lax.dot_general(
            lhs[pl.ds(0, rows_n), pl.ds(0, n_arr)], oh_recv[...], NT, preferred_element_type=F32
        )
        for h in range(rows_n):
            flag = flag_in[:, pl.ds(h * COLS, COLS)].astype(F32)
            code[h : h + 1] = drm[h : h + 1] * (1.0 + flag)
        build_table(code[...], 0)

        def element_codes(i, carry):
            at = pl.ds(pl.multiple_of(i * LANES, LANES), LANES)
            (got,) = look_up(elem[:, at], (0,))
            inn[:, at] = jnp.where(got == 1.0, 1.0, 0.0)
            out[:, at] = jnp.where(got == 2.0, 1.0, 0.0)
            return carry

        lax.fori_loop(0, n_el // LANES, element_codes, 0)

        for j in range(8):
            oh_elem[j] = one_hot_rows(elem[j : j + 1] & (COLS - 1))

        ri = lax.broadcasted_iota(jnp.int32, (16, COLS), 0)
        li = lax.broadcasted_iota(jnp.int32, (16, COLS), 1)
        found = jnp.zeros((16, COLS), F32)
        for h in range(rows_n):
            row = slot[h : h + 1]
            value = jnp.where(ri < 2, h, li)
            hit = ((row >> 8) == (ri & 1)) & (ri < 4)
            found = found + lax.dot_general(
                jnp.where(hit, value, 0).astype(F32).astype(BF16),
                one_hot_rows(row & (COLS - 1)),
                NT,
                preferred_element_type=F32,
            )
        slot_node[...] = jnp.full(slot_node.shape, -1, jnp.int32)
        for r in range(2 * SHARE // LANES):
            at = slice((r % 2) * LANES, (r % 2 + 1) * LANES)
            side = r // 2
            node = found[side : side + 1, at] * COLS + found[2 + side : 3 + side, at]
            slot_node[r : r + 1] = node.astype(jnp.int32)

    def place(k):
        def body(p, carry):
            at = pl.ds(pl.multiple_of(p * LANES, LANES), LANES)
            here = (recv_node[pl.ds(p, 1), :] >> 8) == high_iota
            got = samp_recv[k, p]
            for c in range(3):
                for s, part in enumerate(split(got[c : c + 1])):
                    lhs[pl.ds((2 * c + s) * rows_n, rows_n), at] = jnp.where(
                        here, part, 0.0
                    ).astype(BF16)
            return carry

        lax.fori_loop(0, n_dom, body, 0)
        placed = lax.dot_general(
            lhs[:, pl.ds(0, n_arr)], oh_recv[...], NT, preferred_element_type=F32
        )
        for c in range(3):
            at = 2 * c * rows_n
            free[c] = free[c] + DT * (placed[at : at + rows_n] + placed[at + rows_n : at + 2 * rows_n])

    def element_forces():
        for c in range(3):
            build_table(u_now[c], c)
            build_table(free[c], 3 + c)

        def body(i, carry):
            at = pl.ds(pl.multiple_of(i * LANES, LANES), LANES)
            got = look_up(elem[:, at], range(6))
            inner, outer = inn[:, at], out[:, at]
            blocks = []
            for group in (got[:3], [g * inner for g in got[3:]], [g * outer for g in got[3:]]):
                parts = [split(g) for g in group]
                tops = [t for t, _ in parts]
                blocks += tops + [r for _, r in parts] + tops
            blocks.append(jnp.zeros((8, LANES), F32))
            cols[:, at] = jnp.concatenate(blocks, axis=0).astype(BF16)
            return carry

        lax.fori_loop(0, n_el // LANES, body, 0)
        for part in range(n_el // 512):
            at = pl.ds(part * 512, 512)
            response = jnp.dot(kblock[...], cols[:, at], preferred_element_type=F32)
            inner, outer, mod = inn[:, at], out[:, at], modulus[:, at]
            for c in range(3):
                a = 8 * c
                value = mod * (
                    -response[a : a + 8]
                    + outer * response[24 + a : 32 + a]
                    - inner * response[48 + a : 56 + a]
                )
                fe[0, pl.ds(a, 8), at], fe[1, pl.ds(a, 8), at] = split(value)

        total = jnp.zeros((6 * rows_n, COLS), F32)
        wide_iota = lax.broadcasted_iota(jnp.int32, (rows_n, n_el), 0)
        for j in range(8):
            here = (elem[j : j + 1] >> 8) == wide_iota
            for c in range(3):
                for s in range(2):
                    lhs[pl.ds((2 * c + s) * rows_n, rows_n), pl.ds(0, n_el)] = jnp.where(
                        here, fe[s, 8 * c + j : 8 * c + j + 1], 0.0
                    ).astype(BF16)
            total = total + lax.dot_general(
                lhs[:, pl.ds(0, n_el)], oh_elem[j], NT, preferred_element_type=F32
            )
        for c in range(3):
            at = 2 * c * rows_n
            force[c] = total[at : at + rows_n] + total[at + rows_n : at + 2 * rows_n]

    def rim_copy(k, side):
        there = lax.rem(me_d + (n_dom - 1 if side == 0 else 1), n_dom)
        return pltpu.make_async_remote_copy(
            src_ref=rim_send.at[k, side],
            dst_ref=rim_recv.at[k, 1 - side],
            send_sem=r_send_sem.at[k, side],
            recv_sem=r_recv_sem.at[k, 1 - side],
            device_id=(me_s, there),
            device_id_type=MESH,
        )

    def rim_start(k):
        for c in range(3):
            build_table(force[c], c)
        got = look_up(slot_node[...], range(3))
        for side in range(2):
            for c in range(3):
                rim_send[k, side, 2 * c : 2 * c + 2, :] = got[c][2 * side : 2 * side + 2]
            rim_copy(k, side).start()

    def rim_finish(k):
        for side in range(2):
            rim_copy(k, side).wait_send()
            rim_copy(k, 1 - side).wait_recv()
        for half in range(COLS // LANES):
            at = slice(half * LANES, (half + 1) * LANES)
            index = slot[:, at]
            low, high = index & (LANES - 1), index >> 7
            for c in range(3):
                value = force[c, :, at]
                extra = jnp.zeros(value.shape, F32)
                for r in range(2 * SHARE // LANES):
                    row = rim_recv[k, r // 2, 2 * c + r % 2 : 2 * c + r % 2 + 1, :]
                    got = take_lanes(jnp.broadcast_to(row, index.shape), low)
                    extra = jnp.where(high == r, got, extra)
                u = u_now[c, :, at]
                following = (2.0 * u - u_prev[c, :, at]) + DT_SITE2 * (value + extra) / mass[:, at]
                u_prev[c, :, at] = u
                u_now[c, :, at] = following

    def first_pack(x, carry):
        y_pack(0, STRESS_Y, x, {f: st[f, x + 2] for f, _ in STRESS_Y})
        return carry

    lax.fori_loop(0, cx, first_pack, 0)
    expected = (
        n_dom - 1 + jnp.where(me_s > 0, 1, 0) + jnp.where(me_s < n_site - 1, 1, 0)
    ).astype(jnp.int32)
    pl.semaphore_wait(barrier, expected)
    halo_start(0, STRESS_X, STRESS_Y)
    site_prep()
    for k in range(STEPS):
        halo_wait(0, STRESS_X, STRESS_Y)
        velocity_half()
        halo_start(1, VEL_X, VEL_Y)
        sample(k)
        sample_start(k)
        if k:
            rim_finish(k - 1)
        halo_wait(1, VEL_X, VEL_Y)
        stress_half()
        if k < STEPS - 1:
            halo_start(0, STRESS_X, STRESS_Y)
        else:
            store = pltpu.make_async_copy(st.at[:, pl.ds(2, cx)], basin_out, out_sem)
            store.start()
        sample_wait(k)
        place(k)
        element_forces()
        rim_start(k)
    rim_finish(STEPS - 1)
    for h in range(rows_n):
        for c in range(3):
            disp_out[c : c + 1, pl.ds(h * COLS, COLS)] = u_now[c, h : h + 1]
    store.wait()


def solution(mesh):
    n_site, n_dom = mesh.shape["site"], mesh.shape["dom"]

    def on_device(
        fields, material, send_cell, recv_node, elements, modulus, node_mass, outer_flag, shared_slot, stiffness,
        disp_now, disp_prev,
    ):
        _, cx, cy, nz = fields.shape
        n_nodes = disp_now.shape[3]
        n_el = elements.shape[3]
        rows_n = n_nodes // COLS
        n_arr = n_dom * LANES
        vmem = pl.BlockSpec(memory_space=pltpu.VMEM)
        hbm = pl.BlockSpec(memory_space=pl.ANY)
        sem = pltpu.SemaphoreType.DMA
        node3 = pltpu.VMEM((3, rows_n, COLS), F32)
        basin, disp = pl.pallas_call(
            functools.partial(kernel, n_site, n_dom),
            out_shape=(
                jax.ShapeDtypeStruct(fields.shape, F32),
                jax.ShapeDtypeStruct((3, n_nodes), F32),
            ),
            in_specs=[hbm] + [vmem] * 11,
            out_specs=(hbm, vmem),
            scratch_shapes=[
                pltpu.VMEM((9, cx + 4, cy, nz), F32),
                pltpu.VMEM((2, 6, cx, nz), F32),
                pltpu.VMEM((2, 6, cx, nz), F32),
                pltpu.VMEM((2, 6, cx, nz), F32),
                pltpu.VMEM((2, 6, cx, nz), F32),
                pltpu.VMEM((STEPS, n_dom, 3, LANES), F32),
                pltpu.VMEM((STEPS, n_dom, 3, LANES), F32),
                pltpu.VMEM((STEPS, 2, 8, LANES), F32),
                pltpu.VMEM((STEPS, 2, 8, LANES), F32),
                pltpu.VMEM((COLS, n_arr), BF16),
                pltpu.VMEM((8, COLS, n_el), BF16),
                pltpu.VMEM((6 * rows_n, max(n_el, n_arr)), BF16),
                pltpu.VMEM((6, n_nodes // LANES, 8, LANES), F32),
                pltpu.VMEM((8, n_el), F32),
                pltpu.VMEM((8, n_el), F32),
                pltpu.VMEM((224, n_el), BF16),
                pltpu.VMEM((72, 224), BF16),
                pltpu.VMEM((2, 24, n_el), F32),
                node3,
                node3,
                node3,
                pltpu.VMEM((rows_n, COLS), F32),
                pltpu.VMEM((rows_n, COLS), F32),
                pltpu.VMEM((rows_n, COLS), jnp.int32),
                pltpu.VMEM((8, LANES), jnp.int32),
                node3,
                sem,
                sem,
                sem((2, 2, 3)),
                sem((2, 2, 3)),
                sem((2, 2)),
                sem((2, 2)),
                sem((STEPS, n_dom)),
                sem((STEPS, n_dom)),
                sem((STEPS, 2)),
                sem((STEPS, 2)),
            ],
            compiler_params=pltpu.CompilerParams(
                collective_id=0, has_side_effects=True, vmem_limit_bytes=48 * 1024 * 1024
            ),
        )(
            fields, material, send_cell[0, 0], recv_node[0, 0], elements[0, 0], modulus[0], node_mass[0], outer_flag[0],
            shared_slot[0], stiffness, disp_now[0, 0], disp_prev[0, 0],
        )
        return basin, disp[None, None]

    spread3 = P("site", "dom", None)
    spread4 = P("site", "dom", None, None)
    slab = P(None, "dom", "site", None)
    return jax.shard_map(
        on_device,
        mesh=mesh,
        in_specs=(
            slab, slab, spread4, spread4, spread4, spread3, spread3, spread3, spread3, P(), spread4, spread4,
        ),
        out_specs=(slab, spread4),
        check_vma=False,
    )
```

```python
import functools

import jax
import jax.numpy as jnp
from jax import lax
from jax.experimental import pallas as pl
from jax.experimental.pallas import tpu as pltpu
from jax.sharding import PartitionSpec as P

STEPS = 3
SHARE = 256
C_NEAR = 9.0 / 8.0
C_FAR = 1.0 / 24.0
DT = 0.25
DT_SITE2 = 0.15
MESH = pl.DeviceIdType.MESH
LANES = 128
COLS = 256
F32 = jnp.float32
BF16 = jnp.bfloat16

STRESS_X = ((3, "F"), (6, "B"), (7, "B"))
STRESS_Y = ((6, "B"), (4, "F"), (8, "B"))
VEL_X = ((0, "B"), (1, "F"), (2, "F"))
VEL_Y = ((0, "F"), (1, "B"), (2, "F"))
LOW = {"B": 2, "F": 1}
HIGH = {"B": 1, "F": 2}


def take_lanes(table, lanes):
    return lax.gather(
        table,
        lanes[..., None],
        lax.GatherDimensionNumbers(
            offset_dims=(),
            collapsed_slice_dims=(1,),
            start_index_map=(1,),
            operand_batching_dims=(0,),
            start_indices_batching_dims=(0,),
        ),
        (1, 1),
        mode=lax.GatherScatterMode.PROMISE_IN_BOUNDS,
    )


def stencil(kind, m2, m1, f, p1, p2):
    if kind == "B":
        return C_NEAR * (f - m1) - C_FAR * (p1 - m2)
    return C_NEAR * (p1 - f) - C_FAR * (p2 - m1)


def diff_rolled(kind, f, axis, index, low, high):
    n = f.shape[axis]
    below = lambda v, edge: jnp.where(index == 0, edge, pltpu.roll(v, 1, axis))
    above = lambda v, edge: jnp.where(index == n - 1, edge, pltpu.roll(v, n - 1, axis))
    m1 = below(f, low[-1])
    p1 = above(f, high[0])
    if kind == "B":
        return stencil(kind, below(m1, low[0]), m1, f, p1, None)
    return stencil(kind, None, m1, f, p1, above(p1, high[1]))


def split(v):
    top = v.astype(BF16).astype(F32)
    return top, v - top


def kernel(
    n_site,
    n_dom,
    fields,
    mat_hbm,
    send_cell_hbm,
    recv_node_hbm,
    elem_hbm,
    modulus_hbm,
    mass_in_hbm,
    flag_in_hbm,
    slot_in_hbm,
    stiff_hbm,
    now_in_hbm,
    prev_in_hbm,
    basin_out,
    disp_out,
    mat,
    send_cell,
    recv_node,
    elem,
    modulus,
    mass_in,
    flag_in,
    slot_in,
    stiff,
    now_in,
    prev_in,
    disp_v,
    st,
    y_low,
    y_high,
    y_to_low,
    y_to_high,
    samp_send,
    samp_recv,
    rim_send,
    rim_recv,
    oh_recv,
    oh_recv_t,
    oh_elem,
    oh_elem_t,
    oh_slot,
    oh_slot_t,
    oh_cell,
    high_rows,
    lhs,
    inn,
    out,
    cols,
    kblock,
    node,
    prev,
    slot_node,
    force,
    in_sem,
    out_sem,
    in_sems,
    x_send_sem,
    x_recv_sem,
    y_send_sem,
    y_recv_sem,
    s_send_sem,
    s_recv_sem,
    r_send_sem,
    r_recv_sem,
):
    cx, cy, nz = mat.shape[1:]
    n_nodes = node.shape[1]
    runs = n_nodes // COLS
    n_el = elem.shape[1]
    n_arr = n_dom * LANES
    me_s = lax.axis_index("site")
    me_d = lax.axis_index("dom")

    load = pltpu.make_async_copy(fields, st.at[:, pl.ds(2, cx)], in_sem)
    load.start()
    inputs = [
        pltpu.make_async_copy(src, dst, in_sems.at[i])
        for i, (src, dst) in enumerate(
            (
                (mat_hbm, mat),
                (send_cell_hbm, send_cell),
                (recv_node_hbm, recv_node),
                (elem_hbm, elem),
                (modulus_hbm, modulus),
                (mass_in_hbm, mass_in),
                (flag_in_hbm, flag_in),
                (slot_in_hbm, slot_in),
                (stiff_hbm, stiff),
                (now_in_hbm, now_in),
                (prev_in_hbm, prev_in),
            )
        )
    ]
    for copy in inputs:
        copy.start()
    st[:, pl.ds(0, 2)] = jnp.zeros((9, 2, cy, nz), F32)
    st[:, pl.ds(2 + cx, 2)] = jnp.zeros((9, 2, cy, nz), F32)
    y_low[...] = jnp.zeros(y_low.shape, F32)
    y_high[...] = jnp.zeros(y_high.shape, F32)

    barrier = pltpu.get_barrier_semaphore()

    def greet(d, carry):
        pl.semaphore_signal(
            barrier, inc=1, device_id=(me_s, lax.rem(me_d + d, n_dom)), device_id_type=MESH
        )
        return carry

    lax.fori_loop(1, n_dom, greet, 0)
    for step in (-1, 1):
        there = me_s + step

        @pl.when((there >= 0) & (there < n_site))
        def _():
            pl.semaphore_signal(barrier, inc=1, device_id=(there, me_d), device_id_type=MESH)

    load.wait()
    for copy in inputs:
        copy.wait()

    row_iota = lax.broadcasted_iota(jnp.int32, (cy, nz), 0)
    lane_iota = lax.broadcasted_iota(jnp.int32, (cy, nz), 1)

    def x_copies(which, fields_x, upward):
        made = []
        for at, (f, kind) in enumerate(fields_x):
            if upward:
                width = LOW[kind]
                src = st.at[f, pl.ds(2 + cx - width, width)]
                dst = st.at[f, pl.ds(2 - width, width)]
                there = me_d + 1
            else:
                width = HIGH[kind]
                src = st.at[f, pl.ds(2, width)]
                dst = st.at[f, pl.ds(2 + cx, width)]
                there = me_d - 1
            sem = (which, 1 if upward else 0, at)
            made.append(
                pltpu.make_async_remote_copy(
                    src_ref=src,
                    dst_ref=dst,
                    send_sem=x_send_sem.at[sem],
                    recv_sem=x_recv_sem.at[sem],
                    device_id=(me_s, there),
                    device_id_type=MESH,
                )
            )
        return made

    def y_copy(which, fields_y, upward):
        count = sum((LOW if upward else HIGH)[kind] for _, kind in fields_y)
        src, dst = (y_to_high, y_low) if upward else (y_to_low, y_high)
        sem = (which, 1 if upward else 0)
        return pltpu.make_async_remote_copy(
            src_ref=src.at[which, pl.ds(0, count)],
            dst_ref=dst.at[which, pl.ds(0, count)],
            send_sem=y_send_sem.at[sem],
            recv_sem=y_recv_sem.at[sem],
            device_id=(me_s + (1 if upward else -1), me_d),
            device_id_type=MESH,
        )

    has = {
        "x": (me_d > 0, me_d < n_dom - 1),
        "y": (me_s > 0, me_s < n_site - 1),
    }

    def halo_start(which, fields_x, fields_y):
        for upward in (False, True):

            @pl.when(has["x"][upward])
            def _():
                for copy in x_copies(which, fields_x, upward):
                    copy.start()

            @pl.when(has["y"][upward])
            def _():
                y_copy(which, fields_y, upward).start()

    def halo_wait(which, fields_x, fields_y):
        for upward in (False, True):

            @pl.when(has["x"][upward])
            def _():
                for copy in x_copies(which, fields_x, upward):
                    copy.wait_send()

            @pl.when(has["x"][not upward])
            def _():
                for copy in x_copies(which, fields_x, upward):
                    copy.wait_recv()

            @pl.when(has["y"][upward])
            def _():
                y_copy(which, fields_y, upward).wait_send()

            @pl.when(has["y"][not upward])
            def _():
                y_copy(which, fields_y, upward).wait_recv()

    def y_pack(which, fields_y, x, planes):
        at = 0
        for f, kind in fields_y:
            for k in range(LOW[kind]):
                y = cy - LOW[kind] + k
                y_to_high[which, at, pl.ds(x, 1), :] = planes[f][y : y + 1]
                at += 1
        at = 0
        for f, kind in fields_y:
            for k in range(HIGH[kind]):
                y_to_low[which, at, pl.ds(x, 1), :] = planes[f][k : k + 1]
                at += 1

    def y_edges(which, fields_y, x):
        edges = {}
        low_at = high_at = 0
        for f, kind in fields_y:
            low = [y_low[which, low_at + k, pl.ds(x, 1), :] for k in range(LOW[kind])]
            high = [y_high[which, high_at + k, pl.ds(x, 1), :] for k in range(HIGH[kind])]
            low_at += LOW[kind]
            high_at += HIGH[kind]
            edges[f] = (low, high)
        return edges

    def diff_x(kind, f, x):
        at = lambda o: st[f, x + 2 + o]
        if kind == "B":
            return stencil(kind, at(-2), at(-1), at(0), at(1), None)
        return stencil(kind, None, at(-1), at(0), at(1), at(2))

    def diff_y(kind, f, x, edges):
        low, high = edges[f]
        return diff_rolled(kind, st[f, x + 2], 0, row_iota, low, high)

    def diff_z(kind, f, x):
        return diff_rolled(kind, st[f, x + 2], 1, lane_iota, (0.0, 0.0), (0.0, 0.0))

    def velocity_half():
        def body(x, carry):
            edges = y_edges(0, STRESS_Y, x)
            b = DT * mat[0, x]
            planes = {
                0: st[0, x + 2]
                + b * (diff_x("F", 3, x) + diff_y("B", 6, x, edges) + diff_z("B", 7, x)),
                1: st[1, x + 2]
                + b * (diff_x("B", 6, x) + diff_y("F", 4, x, edges) + diff_z("B", 8, x)),
                2: st[2, x + 2]
                + b * (diff_x("B", 7, x) + diff_y("B", 8, x, edges) + diff_z("F", 5, x)),
            }
            for f, plane in planes.items():
                st[f, x + 2] = plane
            y_pack(1, VEL_Y, x, planes)
            return carry

        lax.fori_loop(0, cx, body, 0)

    def stress_half():
        def body(x, carry):
            edges = y_edges(1, VEL_Y, x)
            lam, mu = mat[1, x], mat[2, x]
            exx = diff_x("B", 0, x)
            eyy = diff_y("B", 1, x, edges)
            ezz = diff_z("B", 2, x)
            wide = lam + 2.0 * mu
            shear = DT * mu
            planes = {
                3: st[3, x + 2] + DT * (wide * exx + lam * (eyy + ezz)),
                4: st[4, x + 2] + DT * (wide * eyy + lam * (exx + ezz)),
                5: st[5, x + 2] + DT * (wide * ezz + lam * (exx + eyy)),
                6: st[6, x + 2] + shear * (diff_y("F", 0, x, edges) + diff_x("F", 1, x)),
                7: st[7, x + 2] + shear * (diff_z("F", 0, x) + diff_x("F", 2, x)),
                8: st[8, x + 2] + shear * (diff_z("F", 1, x) + diff_y("F", 2, x, edges)),
            }
            for f, plane in planes.items():
                st[f, x + 2] = plane
            y_pack(0, STRESS_Y, x, planes)
            return carry

        lax.fori_loop(0, cx, body, 0)

    def sample(k):
        n = n_arr // 2
        for i in range(2):
            cell = [send_cell[q : q + 1] for q in range(i * n_dom // 2, (i + 1) * n_dom // 2)]
            high = jnp.concatenate([jnp.broadcast_to(v >> 8, (8, LANES)) for v in cell], axis=1)
            row = lax.broadcasted_iota(jnp.int32, high.shape, 0)
            for c in range(3):
                parts = split(st[c, pl.ds(2, cx)].reshape(cx * cy, nz))
                table = jnp.concatenate(parts, axis=0).astype(BF16)
                found = jnp.dot(table, oh_cell[:, pl.ds(i * n, n)], preferred_element_type=F32)
                total = jnp.zeros(high.shape, F32)
                for t in range(cx * cy // 8):
                    both = found[8 * t : 8 * t + 8] + found[cx * cy + 8 * t : cx * cy + 8 * t + 8]
                    total = jnp.where(high == row + 8 * t, both, total)
                total = jnp.sum(total, axis=0, keepdims=True)
                for q in range(n_dom // 2):
                    samp_send[k, i * n_dom // 2 + q, c : c + 1, :] = total[
                        :, q * LANES : (q + 1) * LANES
                    ]

    def sample_copy(k, d):
        there = lax.rem(me_d + d, n_dom)
        return pltpu.make_async_remote_copy(
            src_ref=samp_send.at[k, there],
            dst_ref=samp_recv.at[k, me_d],
            send_sem=s_send_sem.at[k, d],
            recv_sem=s_recv_sem.at[k, d],
            device_id=(me_s, there),
            device_id_type=MESH,
        )

    def sample_start(k):
        def body(d, carry):
            sample_copy(k, d).start()
            return carry

        lax.fori_loop(1, n_dom, body, 0)
        samp_recv[k, me_d] = samp_send[k, me_d]

    def sample_wait(k):
        def body(d, carry):
            here = lax.rem(me_d + n_dom - d, n_dom)
            copy = pltpu.make_async_remote_copy(
                src_ref=samp_send.at[k, here],
                dst_ref=samp_recv.at[k, here],
                send_sem=s_send_sem.at[k, d],
                recv_sem=s_recv_sem.at[k, d],
                device_id=(me_s, here),
                device_id_type=MESH,
            )
            copy.wait_recv()
            sample_copy(k, d).wait_send()
            return carry

        lax.fori_loop(1, n_dom, body, 0)

    def run(h):
        return pl.ds(h * COLS, COLS)

    def by_run(value):
        return jnp.concatenate([value[:, h * COLS : (h + 1) * COLS] for h in range(runs)], axis=0)

    def by_node(value):
        return jnp.concatenate([value[8 * h : 8 * h + 8] for h in range(runs)], axis=1)

    def packed(row):
        return jnp.broadcast_to(row.astype(F32), (16, row.shape[1])).astype(BF16)

    def one_hot(low, ref):
        low16 = packed(low)
        iota = lax.broadcasted_iota(jnp.int32, low16.shape, 0).astype(F32).astype(BF16)
        one, zero = jnp.ones(low16.shape, BF16), jnp.zeros(low16.shape, BF16)
        for t in range(COLS // 16):
            ref[pl.ds(16 * t, 16), :] = jnp.where(iota + BF16(16 * t) == low16, one, zero)

    def one_hot_both(low, ref, turned):
        one_hot(low, ref)
        turned[...] = ref[...].T

    def spread(high, values, ref):
        high16 = packed(high)
        twice = jnp.concatenate([values, values], axis=0).astype(BF16)
        second = (lax.broadcasted_iota(jnp.int32, high16.shape, 0) >> 3).astype(F32).astype(BF16)
        zero = jnp.zeros(high16.shape, BF16)
        for t in range(runs // 2):
            ref[pl.ds(16 * t, 16), :] = jnp.where(second + BF16(2 * t) == high16, twice, zero)

    def sub(shape):
        return lax.broadcasted_iota(jnp.int32, shape, 0) & 7

    def prep_nodes():
        node[...] = jnp.zeros(node.shape, F32)
        prev[...] = jnp.zeros(prev.shape, F32)
        for c in range(3):
            node[c : c + 1, :] = now_in[c]
            prev[c : c + 1, :] = prev_in[c]

    def prep_k():
        n_k = stiff.shape[0]
        n_r, n_c = kblock.shape

        def dof(i, comp):
            return comp * 8 + ((i & 63) >> 3)

        def comp3(i):
            r = i & 7
            return jnp.where(r < 3, r, r - 3)

        ri = lax.broadcasted_iota(jnp.int32, (n_r, n_k), 0)
        rk = lax.broadcasted_iota(jnp.int32, (n_r, n_k), 1)
        pick_r = jnp.where((dof(ri, comp3(ri)) == rk) & ((ri & 7) < 6), 1.0, 0.0)
        ck = lax.broadcasted_iota(jnp.int32, (n_k, n_c), 0)
        ci = lax.broadcasted_iota(jnp.int32, (n_k, n_c), 1)
        pick_c = jnp.where((dof(ci, comp3(ci)) == ck) & ((ci & 7) < 6), 1.0, 0.0)
        exact = functools.partial(
            jnp.dot, precision=lax.Precision.HIGHEST, preferred_element_type=F32
        )
        top, rest = split(exact(exact(pick_r, stiff[...]), pick_c))
        group = lax.broadcasted_iota(jnp.int32, (n_r, n_c), 0) >> 6
        ci = lax.broadcasted_iota(jnp.int32, (n_r, n_c), 1)
        block, free_col = ci >> 6, (ci & 7) >= 3
        outer_block = (block == 2) | (block == 3) | (block == 5)
        inner_block = (block == 0) | (block == 1) | (block == 4)
        meant = (
            ((group == 0) & ((ci & 7) < 3) & inner_block)
            | ((group == 1) & free_col & inner_block)
            | ((group == 2) & free_col & outer_block)
        )
        value = jnp.where(block >= 4, rest, top)
        value = jnp.where(group == 1, value, -value)
        kblock[...] = jnp.where(meant, value, 0.0).astype(BF16)

    def prep_arr():
        for p in range(n_dom):
            at = pl.ds(p * LANES, LANES)
            one_hot_both(recv_node[p : p + 1] & (COLS - 1), oh_recv.at[:, at], oh_recv_t.at[at])

    def prep_hot():
        for j in range(8):
            one_hot_both(elem[j : j + 1] & (COLS - 1), oh_elem.at[j], oh_elem_t.at[j])
            high_rows[j] = jnp.broadcast_to(elem[j : j + 1] >> 8, (8, n_el))

    def prep_cell():
        for q in range(n_dom):
            one_hot(send_cell[q : q + 1] & (nz - 1), oh_cell.at[:, pl.ds(q * LANES, LANES)])

    def prep_slot():
        row = slot_in[...]
        one_hot_both(row & (COLS - 1), oh_slot, oh_slot_t)
        ri = lax.broadcasted_iota(jnp.int32, (16, n_nodes), 0)
        li = lax.broadcasted_iota(jnp.int32, (16, n_nodes), 1)
        value = jnp.where(ri < 2, li >> 8, li & (COLS - 1))
        hit = ((row >> 8) == (ri & 1)) & (ri < 4)
        found = jnp.dot(
            jnp.where(hit, value, 0).astype(F32).astype(BF16),
            oh_slot_t[...],
            preferred_element_type=F32,
        )
        for r in range(2 * SHARE // LANES):
            at = slice((r % 2) * LANES, (r % 2 + 1) * LANES)
            side = r // 2
            where = found[side : side + 1, at] * COLS + found[2 + side : 3 + side, at]
            slot_node[r] = jnp.broadcast_to(where.astype(jnp.int32), (8, LANES))

    def place(k):
        for p in range(n_dom):
            got = samp_recv[k, p]
            top, rest = split(got)
            values = jnp.concatenate([rest, top, jnp.ones((2, LANES), F32)], axis=0)
            spread(recv_node[p : p + 1] >> 8, values, lhs.at[0, :, pl.ds(p * LANES, LANES)])
        placed = by_node(
            jnp.dot(lhs[0, :, pl.ds(0, n_arr)], oh_recv_t[...], preferred_element_type=F32)
        )
        old, row = node[...], sub(node.shape)
        both = placed + pltpu.roll(placed, 3, 0)
        new = jnp.where((row >= 3) & (row < 6), old + DT * both, old)
        if k == 0:
            flag = flag_in[...].astype(F32)
            share = jnp.where(row == 7, flag, 1.0 - flag)
            new = jnp.where(row >= 6, placed * share, new)
        node[...] = new

    def element_cols(k):
        top, rest = split(by_run(node[...]))
        table = jnp.concatenate([top, rest], axis=0).astype(BF16)
        first = sub((8, COLS)) < 3
        for i in range(n_el // COLS):
            at = pl.ds(i * COLS, COLS)
            for pair in range(4):
                with_inner, with_outer = [], []
                for j in (2 * pair, 2 * pair + 1):
                    found = jnp.dot(table, oh_elem[j, :, at], preferred_element_type=F32)
                    high = high_rows[j, :, at]
                    got = jnp.zeros((8, COLS), F32)
                    for h in range(runs):
                        both = found[8 * h : 8 * h + 8] + found[8 * (runs + h) : 8 * (runs + h) + 8]
                        got = jnp.where(high == h, both, got)
                    if k == 0:
                        inn[j, :, at] = jnp.broadcast_to(got[6:7], got.shape)
                        out[j, :, at] = jnp.broadcast_to(got[7:8], got.shape)
                    with_inner.append(jnp.where(first, got, got * inn[j, :, at]))
                    with_outer.append(got * out[j, :, at])
                blocks = split(jnp.concatenate(with_inner, axis=0))
                blocks += split(jnp.concatenate(with_outer, axis=0))
                blocks += (blocks[0], blocks[2])
                for which, block in enumerate(blocks):
                    cols[pl.ds(64 * which + 16 * pair, 16), at] = block.astype(BF16)

    def element_response():
        wide = n_el // 2
        first = sub((8, wide)) < 3
        for i in range(2):
            at = pl.ds(i * wide, wide)
            response = jnp.dot(kblock[...], cols[:, at], preferred_element_type=F32)
            mod = jnp.broadcast_to(modulus[:, at], (8, wide))
            for j in range(8):
                value = mod * (
                    response[8 * j : 8 * j + 8]
                    + out[j, :, at] * response[64 + 8 * j : 72 + 8 * j]
                    + inn[j, :, at] * response[128 + 8 * j : 136 + 8 * j]
                )
                top, rest = split(value)
                spread(elem[j : j + 1, at] >> 8, jnp.where(first, top, rest), lhs.at[j, :, at])

    def element_add():
        total = jnp.zeros((8 * runs, COLS), F32)
        for j in range(8):
            total = total + jnp.dot(
                lhs[j, :, pl.ds(0, n_el)], oh_elem_t[j], preferred_element_type=F32
            )
        both = by_node(total)
        force[...] = both + pltpu.roll(both, 5, 0)

    def rim_copy(k, side):
        there = lax.rem(me_d + (n_dom - 1 if side == 0 else 1), n_dom)
        return pltpu.make_async_remote_copy(
            src_ref=rim_send.at[k, side],
            dst_ref=rim_recv.at[k, 1 - side],
            send_sem=r_send_sem.at[k, side],
            recv_sem=r_recv_sem.at[k, 1 - side],
            device_id=(me_s, there),
            device_id_type=MESH,
        )

    def rim_start(k):
        for side in range(2):
            for half in range(SHARE // LANES):
                index = slot_node[2 * side + half]
                low, high = index & (LANES - 1), index >> 7
                got = jnp.zeros((8, LANES), F32)
                for r in range(n_nodes // LANES):
                    piece = take_lanes(force[:, pl.ds(r * LANES, LANES)], low)
                    got = jnp.where(high == r, piece, got)
                rim_send[k, side, :, pl.ds(half * LANES, LANES)] = got[:3]
            rim_copy(k, side).start()

    def rim_finish(k):
        for side in range(2):
            rim_copy(k, side).wait_send()
            rim_copy(k, 1 - side).wait_recv()
        tables = []
        for r in range(2 * SHARE // LANES):
            got = rim_recv[k, r // 2, :, pl.ds((r % 2) * LANES, LANES)]
            tables.append(jnp.concatenate([got, jnp.zeros((5, LANES), F32)], axis=0))
        for i in range(n_nodes // LANES):
            at = pl.ds(i * LANES, LANES)
            index = jnp.broadcast_to(slot_in[:, at], (8, LANES))
            low, high = index & (LANES - 1), index >> 7
            extra = jnp.zeros((8, LANES), F32)
            for r, piece in enumerate(tables):
                extra = jnp.where(high == r, take_lanes(piece, low), extra)
            u = node[:, at]
            following = (2.0 * u - prev[:, at]) + DT_SITE2 * (force[:, at] + extra) / mass_in[:, at]
            prev[:, at] = u
            node[:, at] = jnp.where(sub(u.shape) < 3, following, u)

    def first_pack(x, carry):
        y_pack(0, STRESS_Y, x, {f: st[f, x + 2] for f, _ in STRESS_Y})
        return carry

    lax.fori_loop(0, cx, first_pack, 0)
    expected = (
        n_dom - 1 + jnp.where(me_s > 0, 1, 0) + jnp.where(me_s < n_site - 1, 1, 0)
    ).astype(jnp.int32)
    pl.semaphore_wait(barrier, expected)
    halo_start(0, STRESS_X, STRESS_Y)
    prep_nodes()
    prep_k()
    prep_arr()
    prep_hot()
    prep_slot()
    prep_cell()
    for k in range(STEPS):
        halo_wait(0, STRESS_X, STRESS_Y)
        velocity_half()
        halo_start(1, VEL_X, VEL_Y)
        sample(k)
        sample_start(k)
        if k:
            rim_finish(k - 1)
        halo_wait(1, VEL_X, VEL_Y)
        stress_half()
        if k < STEPS - 1:
            halo_start(0, STRESS_X, STRESS_Y)
        else:
            store = pltpu.make_async_copy(st.at[:, pl.ds(2, cx)], basin_out, out_sem)
            store.start()
        sample_wait(k)
        place(k)
        element_cols(k)
        element_response()
        element_add()
        rim_start(k)
    rim_finish(STEPS - 1)
    for c in range(3):
        disp_v[c] = node[c : c + 1, :]
    disp_store = pltpu.make_async_copy(disp_v, disp_out, in_sem)
    disp_store.start()
    disp_store.wait()
    store.wait()


def solution(mesh):
    n_site, n_dom = mesh.shape["site"], mesh.shape["dom"]

    def on_device(
        fields, material, send_cell, recv_node, elements, modulus, node_mass, outer_flag, shared_slot, stiffness,
        disp_now, disp_prev,
    ):
        _, cx, cy, nz = fields.shape
        n_nodes = disp_now.shape[3]
        n_el = elements.shape[3]
        runs = n_nodes // COLS
        n_arr = n_dom * LANES
        hbm = pl.BlockSpec(memory_space=pltpu.HBM)
        sem = pltpu.SemaphoreType.DMA
        operands = (
            fields, material, send_cell[0, 0], recv_node[0, 0], elements[0, 0], modulus[0], node_mass[0], outer_flag[0],
            shared_slot[0], stiffness, disp_now.reshape(3, 1, n_nodes), disp_prev.reshape(3, 1, n_nodes),
        )
        basin, disp = pl.pallas_call(
            functools.partial(kernel, n_site, n_dom),
            out_shape=(
                jax.ShapeDtypeStruct(fields.shape, F32),
                jax.ShapeDtypeStruct((3, 1, n_nodes), F32),
            ),
            in_specs=[hbm] * 12,
            out_specs=(hbm, hbm),
            scratch_shapes=[
                *(pltpu.VMEM(v.shape, v.dtype) for v in operands[1:]),
                pltpu.VMEM((3, 1, n_nodes), F32),
                pltpu.VMEM((9, cx + 4, cy, nz), F32),
                pltpu.VMEM((2, 6, cx, nz), F32),
                pltpu.VMEM((2, 6, cx, nz), F32),
                pltpu.VMEM((2, 6, cx, nz), F32),
                pltpu.VMEM((2, 6, cx, nz), F32),
                pltpu.VMEM((STEPS, n_dom, 3, LANES), F32),
                pltpu.VMEM((STEPS, n_dom, 3, LANES), F32),
                pltpu.VMEM((STEPS, 2, 3, SHARE), F32),
                pltpu.VMEM((STEPS, 2, 3, SHARE), F32),
                pltpu.VMEM((COLS, n_arr), BF16),
                pltpu.VMEM((n_arr, COLS), BF16),
                pltpu.VMEM((8, COLS, n_el), BF16),
                pltpu.VMEM((8, n_el, COLS), BF16),
                pltpu.VMEM((COLS, n_nodes), BF16),
                pltpu.VMEM((n_nodes, COLS), BF16),
                pltpu.VMEM((nz, n_arr), BF16),
                pltpu.VMEM((8, 8, n_el), jnp.int32),
                pltpu.VMEM((8, 8 * runs, max(n_el, n_arr)), BF16),
                pltpu.VMEM((8, 8, n_el), F32),
                pltpu.VMEM((8, 8, n_el), F32),
                pltpu.VMEM((384, n_el), BF16),
                pltpu.VMEM((192, 384), BF16),
                pltpu.VMEM((8, n_nodes), F32),
                pltpu.VMEM((8, n_nodes), F32),
                pltpu.VMEM((2 * SHARE // LANES, 8, LANES), jnp.int32),
                pltpu.VMEM((8, n_nodes), F32),
                sem,
                sem,
                sem((11,)),
                sem((2, 2, 3)),
                sem((2, 2, 3)),
                sem((2, 2)),
                sem((2, 2)),
                sem((STEPS, n_dom)),
                sem((STEPS, n_dom)),
                sem((STEPS, 2)),
                sem((STEPS, 2)),
            ],
            compiler_params=pltpu.CompilerParams(
                collective_id=0, has_side_effects=True, vmem_limit_bytes=62 * 1024 * 1024
            ),
        )(*operands)
        return basin, disp.reshape(disp_now.shape)

    spread3 = P("site", "dom", None)
    spread4 = P("site", "dom", None, None)
    slab = P(None, "dom", "site", None)
    return jax.shard_map(
        on_device,
        mesh=mesh,
        in_specs=(
            slab, slab, spread4, spread4, spread4, spread3, spread3, spread3, spread3, P(), spread4, spread4,
        ),
        out_specs=(slab, spread4),
        check_vma=False,
    )
```

```python
import functools

import jax
import jax.numpy as jnp
from jax import lax
from jax.experimental import pallas as pl
from jax.experimental.pallas import tpu as pltpu
from jax.sharding import PartitionSpec as P

STEPS = 3
SHARE = 256
C_NEAR = 9.0 / 8.0
C_FAR = 1.0 / 24.0
DT = 0.25
DT_SITE2 = 0.15
MESH = pl.DeviceIdType.MESH
LANES = 128
COLS = 256
F32 = jnp.float32
BF16 = jnp.bfloat16

STRESS_X = ((3, "F"), (6, "B"), (7, "B"))
STRESS_Y = ((6, "B"), (4, "F"), (8, "B"))
VEL_X = ((0, "B"), (1, "F"), (2, "F"))
VEL_Y = ((0, "F"), (1, "B"), (2, "F"))
LOW = {"B": 2, "F": 1}
HIGH = {"B": 1, "F": 2}


def take_lanes(table, lanes):
    return lax.gather(
        table,
        lanes[..., None],
        lax.GatherDimensionNumbers(
            offset_dims=(),
            collapsed_slice_dims=(1,),
            start_index_map=(1,),
            operand_batching_dims=(0,),
            start_indices_batching_dims=(0,),
        ),
        (1, 1),
        mode=lax.GatherScatterMode.PROMISE_IN_BOUNDS,
    )


def stencil(kind, m2, m1, f, p1, p2):
    if kind == "B":
        return C_NEAR * (f - m1) - C_FAR * (p1 - m2)
    return C_NEAR * (p1 - f) - C_FAR * (p2 - m1)


def diff_rolled(kind, f, axis, index, low, high):
    n = f.shape[axis]
    below = lambda v, edge: jnp.where(index == 0, edge, pltpu.roll(v, 1, axis))
    above = lambda v, edge: jnp.where(index == n - 1, edge, pltpu.roll(v, n - 1, axis))
    m1 = below(f, low[-1])
    p1 = above(f, high[0])
    if kind == "B":
        return stencil(kind, below(m1, low[0]), m1, f, p1, None)
    return stencil(kind, None, m1, f, p1, above(p1, high[1]))


def split(v):
    top = v.astype(BF16).astype(F32)
    return top, v - top


def kernel(
    n_site,
    n_dom,
    fields,
    mat_hbm,
    send_cell_hbm,
    recv_node_hbm,
    elem_hbm,
    modulus_hbm,
    mass_in_hbm,
    flag_in_hbm,
    slot_in_hbm,
    stiff_hbm,
    now_in_hbm,
    prev_in_hbm,
    basin_out,
    disp_out,
    mat,
    send_cell,
    recv_node,
    elem,
    modulus,
    mass_in,
    flag_in,
    slot_in,
    stiff,
    now_in,
    prev_in,
    disp_v,
    st,
    y_low,
    y_high,
    y_to_low,
    y_to_high,
    samp_send,
    samp_recv,
    rim_send,
    rim_recv,
    oh_recv,
    oh_recv_t,
    oh_elem,
    oh_elem_t,
    oh_slot,
    oh_slot_t,
    oh_cell,
    high_rows,
    lhs,
    inn,
    out,
    cols,
    kblock,
    node,
    prev,
    slot_node,
    force,
    in_sem,
    out_sem,
    in_sems,
    x_send_sem,
    x_recv_sem,
    y_send_sem,
    y_recv_sem,
    s_send_sem,
    s_recv_sem,
    r_send_sem,
    r_recv_sem,
):
    cx, cy, nz = mat.shape[1:]
    n_nodes = node.shape[1]
    runs = n_nodes // COLS
    n_el = elem.shape[1]
    n_arr = n_dom * LANES
    me_s = lax.axis_index("site")
    me_d = lax.axis_index("dom")

    load = pltpu.make_async_copy(fields, st.at[:, pl.ds(2, cx)], in_sem)
    load.start()
    inputs = [
        pltpu.make_async_copy(src, dst, in_sems.at[i])
        for i, (src, dst) in enumerate(
            (
                (mat_hbm, mat),
                (send_cell_hbm, send_cell),
                (recv_node_hbm, recv_node),
                (elem_hbm, elem),
                (modulus_hbm, modulus),
                (mass_in_hbm, mass_in),
                (flag_in_hbm, flag_in),
                (slot_in_hbm, slot_in),
                (stiff_hbm, stiff),
                (now_in_hbm, now_in),
                (prev_in_hbm, prev_in),
            )
        )
    ]
    for copy in inputs:
        copy.start()
    st[:, pl.ds(0, 2)] = jnp.zeros((9, 2, cy, nz), F32)
    st[:, pl.ds(2 + cx, 2)] = jnp.zeros((9, 2, cy, nz), F32)
    y_low[...] = jnp.zeros(y_low.shape, F32)
    y_high[...] = jnp.zeros(y_high.shape, F32)

    barrier = pltpu.get_barrier_semaphore()

    def greet(d, carry):
        pl.semaphore_signal(
            barrier, inc=1, device_id=(me_s, lax.rem(me_d + d, n_dom)), device_id_type=MESH
        )
        return carry

    lax.fori_loop(1, n_dom, greet, 0)
    for step in (-1, 1):
        there = me_s + step

        @pl.when((there >= 0) & (there < n_site))
        def _():
            pl.semaphore_signal(barrier, inc=1, device_id=(there, me_d), device_id_type=MESH)

    load.wait()
    for copy in inputs:
        copy.wait()

    row_iota = lax.broadcasted_iota(jnp.int32, (cy, nz), 0)
    lane_iota = lax.broadcasted_iota(jnp.int32, (cy, nz), 1)

    def x_copies(which, fields_x, upward):
        made = []
        for at, (f, kind) in enumerate(fields_x):
            if upward:
                width = LOW[kind]
                src = st.at[f, pl.ds(2 + cx - width, width)]
                dst = st.at[f, pl.ds(2 - width, width)]
                there = me_d + 1
            else:
                width = HIGH[kind]
                src = st.at[f, pl.ds(2, width)]
                dst = st.at[f, pl.ds(2 + cx, width)]
                there = me_d - 1
            sem = (which, 1 if upward else 0, at)
            made.append(
                pltpu.make_async_remote_copy(
                    src_ref=src,
                    dst_ref=dst,
                    send_sem=x_send_sem.at[sem],
                    recv_sem=x_recv_sem.at[sem],
                    device_id=(me_s, there),
                    device_id_type=MESH,
                )
            )
        return made

    def y_copy(which, fields_y, upward):
        count = sum((LOW if upward else HIGH)[kind] for _, kind in fields_y)
        src, dst = (y_to_high, y_low) if upward else (y_to_low, y_high)
        sem = (which, 1 if upward else 0)
        return pltpu.make_async_remote_copy(
            src_ref=src.at[which, pl.ds(0, count)],
            dst_ref=dst.at[which, pl.ds(0, count)],
            send_sem=y_send_sem.at[sem],
            recv_sem=y_recv_sem.at[sem],
            device_id=(me_s + (1 if upward else -1), me_d),
            device_id_type=MESH,
        )

    has = {
        "x": (me_d > 0, me_d < n_dom - 1),
        "y": (me_s > 0, me_s < n_site - 1),
    }

    def halo_start(which, fields_x, fields_y):
        for upward in (False, True):

            @pl.when(has["x"][upward])
            def _():
                for copy in x_copies(which, fields_x, upward):
                    copy.start()

            @pl.when(has["y"][upward])
            def _():
                y_copy(which, fields_y, upward).start()

    def halo_wait(which, fields_x, fields_y):
        for upward in (False, True):

            @pl.when(has["x"][upward])
            def _():
                for copy in x_copies(which, fields_x, upward):
                    copy.wait_send()

            @pl.when(has["x"][not upward])
            def _():
                for copy in x_copies(which, fields_x, upward):
                    copy.wait_recv()

            @pl.when(has["y"][upward])
            def _():
                y_copy(which, fields_y, upward).wait_send()

            @pl.when(has["y"][not upward])
            def _():
                y_copy(which, fields_y, upward).wait_recv()

    def y_pack(which, fields_y, x, planes):
        at = 0
        for f, kind in fields_y:
            for k in range(LOW[kind]):
                y = cy - LOW[kind] + k
                y_to_high[which, at, x : x + 1, :] = planes[f][y : y + 1]
                at += 1
        at = 0
        for f, kind in fields_y:
            for k in range(HIGH[kind]):
                y_to_low[which, at, x : x + 1, :] = planes[f][k : k + 1]
                at += 1

    def y_edges(which, fields_y, x):
        edges = {}
        low_at = high_at = 0
        for f, kind in fields_y:
            low = [y_low[which, low_at + k, x : x + 1, :] for k in range(LOW[kind])]
            high = [y_high[which, high_at + k, x : x + 1, :] for k in range(HIGH[kind])]
            low_at += LOW[kind]
            high_at += HIGH[kind]
            edges[f] = (low, high)
        return edges

    def diff_x(kind, f, x):
        at = lambda o: st[f, x + 2 + o]
        if kind == "B":
            return stencil(kind, at(-2), at(-1), at(0), at(1), None)
        return stencil(kind, None, at(-1), at(0), at(1), at(2))

    def diff_y(kind, f, x, edges):
        low, high = edges[f]
        return diff_rolled(kind, st[f, x + 2], 0, row_iota, low, high)

    def diff_z(kind, f, x):
        return diff_rolled(kind, st[f, x + 2], 1, lane_iota, (0.0, 0.0), (0.0, 0.0))

    def velocity_half():
        def body(x):
            edges = y_edges(0, STRESS_Y, x)
            b = DT * mat[0, x]
            planes = {
                0: st[0, x + 2]
                + b * (diff_x("F", 3, x) + diff_y("B", 6, x, edges) + diff_z("B", 7, x)),
                1: st[1, x + 2]
                + b * (diff_x("B", 6, x) + diff_y("F", 4, x, edges) + diff_z("B", 8, x)),
                2: st[2, x + 2]
                + b * (diff_x("B", 7, x) + diff_y("B", 8, x, edges) + diff_z("F", 5, x)),
            }
            for f, plane in planes.items():
                st[f, x + 2] = plane
            y_pack(1, VEL_Y, x, planes)

        for x in range(cx):
            body(x)

    def stress_half():
        def body(x):
            edges = y_edges(1, VEL_Y, x)
            lam, mu = mat[1, x], mat[2, x]
            exx = diff_x("B", 0, x)
            eyy = diff_y("B", 1, x, edges)
            ezz = diff_z("B", 2, x)
            wide = lam + 2.0 * mu
            shear = DT * mu
            planes = {
                3: st[3, x + 2] + DT * (wide * exx + lam * (eyy + ezz)),
                4: st[4, x + 2] + DT * (wide * eyy + lam * (exx + ezz)),
                5: st[5, x + 2] + DT * (wide * ezz + lam * (exx + eyy)),
                6: st[6, x + 2] + shear * (diff_y("F", 0, x, edges) + diff_x("F", 1, x)),
                7: st[7, x + 2] + shear * (diff_z("F", 0, x) + diff_x("F", 2, x)),
                8: st[8, x + 2] + shear * (diff_z("F", 1, x) + diff_y("F", 2, x, edges)),
            }
            for f, plane in planes.items():
                st[f, x + 2] = plane
            y_pack(0, STRESS_Y, x, planes)

        for x in range(cx):
            body(x)

    def sample(k):
        n = n_arr // 2
        for i in range(2):
            cell = [send_cell[q : q + 1] for q in range(i * n_dom // 2, (i + 1) * n_dom // 2)]
            high = jnp.concatenate([jnp.broadcast_to(v >> 8, (8, LANES)) for v in cell], axis=1)
            row = lax.broadcasted_iota(jnp.int32, high.shape, 0)
            for c in range(3):
                parts = split(st[c, pl.ds(2, cx)].reshape(cx * cy, nz))
                table = jnp.concatenate(parts, axis=0).astype(BF16)
                found = jnp.dot(table, oh_cell[:, pl.ds(i * n, n)], preferred_element_type=F32)
                total = jnp.zeros(high.shape, F32)
                for t in range(cx * cy // 8):
                    both = found[8 * t : 8 * t + 8] + found[cx * cy + 8 * t : cx * cy + 8 * t + 8]
                    total = jnp.where(high == row + 8 * t, both, total)
                total = jnp.sum(total, axis=0, keepdims=True)
                for q in range(n_dom // 2):
                    samp_send[k, i * n_dom // 2 + q, c : c + 1, :] = total[
                        :, q * LANES : (q + 1) * LANES
                    ]

    def sample_copy(k, d):
        there = lax.rem(me_d + d, n_dom)
        return pltpu.make_async_remote_copy(
            src_ref=samp_send.at[k, there],
            dst_ref=samp_recv.at[k, me_d],
            send_sem=s_send_sem.at[k, d],
            recv_sem=s_recv_sem.at[k, d],
            device_id=(me_s, there),
            device_id_type=MESH,
        )

    def sample_start(k):
        for d in range(1, n_dom):
            sample_copy(k, d).start()
        samp_recv[k, me_d] = samp_send[k, me_d]

    def sample_wait(k):
        for d in range(1, n_dom):
            here = lax.rem(me_d + n_dom - d, n_dom)
            copy = pltpu.make_async_remote_copy(
                src_ref=samp_send.at[k, here],
                dst_ref=samp_recv.at[k, here],
                send_sem=s_send_sem.at[k, d],
                recv_sem=s_recv_sem.at[k, d],
                device_id=(me_s, here),
                device_id_type=MESH,
            )
            copy.wait_recv()
            sample_copy(k, d).wait_send()

    def run(h):
        return pl.ds(h * COLS, COLS)

    def by_run(value):
        return jnp.concatenate([value[:, h * COLS : (h + 1) * COLS] for h in range(runs)], axis=0)

    def by_node(value):
        return jnp.concatenate([value[8 * h : 8 * h + 8] for h in range(runs)], axis=1)

    def packed(row):
        return jnp.broadcast_to(row.astype(F32), (16, row.shape[1])).astype(BF16)

    def one_hot(low, ref):
        low16 = packed(low)
        iota = lax.broadcasted_iota(jnp.int32, low16.shape, 0).astype(F32).astype(BF16)
        one, zero = jnp.ones(low16.shape, BF16), jnp.zeros(low16.shape, BF16)
        for t in range(COLS // 16):
            ref[pl.ds(16 * t, 16), :] = jnp.where(iota + BF16(16 * t) == low16, one, zero)

    def one_hot_both(low, ref, turned):
        one_hot(low, ref)
        turned[...] = ref[...].T

    def spread(high, values, ref):
        high16 = packed(high)
        twice = jnp.concatenate([values, values], axis=0).astype(BF16)
        second = (lax.broadcasted_iota(jnp.int32, high16.shape, 0) >> 3).astype(F32).astype(BF16)
        zero = jnp.zeros(high16.shape, BF16)
        for t in range(runs // 2):
            ref[pl.ds(16 * t, 16), :] = jnp.where(second + BF16(2 * t) == high16, twice, zero)

    def sub(shape):
        return lax.broadcasted_iota(jnp.int32, shape, 0) & 7

    def prep_nodes():
        node[...] = jnp.zeros(node.shape, F32)
        prev[...] = jnp.zeros(prev.shape, F32)
        for c in range(3):
            node[c : c + 1, :] = now_in[c]
            prev[c : c + 1, :] = prev_in[c]

    def prep_k():
        n_k = stiff.shape[0]
        n_r, n_c = kblock.shape

        def dof(i, comp):
            return comp * 8 + ((i & 63) >> 3)

        def comp3(i):
            r = i & 7
            return jnp.where(r < 3, r, r - 3)

        ri = lax.broadcasted_iota(jnp.int32, (n_r, n_k), 0)
        rk = lax.broadcasted_iota(jnp.int32, (n_r, n_k), 1)
        pick_r = jnp.where((dof(ri, comp3(ri)) == rk) & ((ri & 7) < 6), 1.0, 0.0)
        ck = lax.broadcasted_iota(jnp.int32, (n_k, n_c), 0)
        ci = lax.broadcasted_iota(jnp.int32, (n_k, n_c), 1)
        pick_c = jnp.where((dof(ci, comp3(ci)) == ck) & ((ci & 7) < 6), 1.0, 0.0)
        exact = functools.partial(
            jnp.dot, precision=lax.Precision.HIGHEST, preferred_element_type=F32
        )
        top, rest = split(exact(exact(pick_r, stiff[...]), pick_c))
        group = lax.broadcasted_iota(jnp.int32, (n_r, n_c), 0) >> 6
        ci = lax.broadcasted_iota(jnp.int32, (n_r, n_c), 1)
        block, free_col = ci >> 6, (ci & 7) >= 3
        outer_block = (block == 2) | (block == 3) | (block == 5)
        inner_block = (block == 0) | (block == 1) | (block == 4)
        meant = (
            ((group == 0) & ((ci & 7) < 3) & inner_block)
            | ((group == 1) & free_col & inner_block)
            | ((group == 2) & free_col & outer_block)
        )
        value = jnp.where(block >= 4, rest, top)
        value = jnp.where(group == 1, value, -value)
        kblock[...] = jnp.where(meant, value, 0.0).astype(BF16)

    def prep_arr():
        for p in range(n_dom):
            at = pl.ds(p * LANES, LANES)
            one_hot_both(recv_node[p : p + 1] & (COLS - 1), oh_recv.at[:, at], oh_recv_t.at[at])

    def prep_hot():
        for j in range(8):
            one_hot_both(elem[j : j + 1] & (COLS - 1), oh_elem.at[j], oh_elem_t.at[pl.ds(j * n_el, n_el)])
            high_rows[j] = jnp.broadcast_to(elem[j : j + 1] >> 8, (8, n_el))

    def prep_cell():
        for q in range(n_dom):
            one_hot(send_cell[q : q + 1] & (nz - 1), oh_cell.at[:, pl.ds(q * LANES, LANES)])

    def prep_slot():
        row = slot_in[...]
        one_hot_both(row & (COLS - 1), oh_slot, oh_slot_t)
        ri = lax.broadcasted_iota(jnp.int32, (16, n_nodes), 0)
        li = lax.broadcasted_iota(jnp.int32, (16, n_nodes), 1)
        value = jnp.where(ri < 2, li >> 8, li & (COLS - 1))
        hit = ((row >> 8) == (ri & 1)) & (ri < 4)
        found = jnp.dot(
            jnp.where(hit, value, 0).astype(F32).astype(BF16),
            oh_slot_t[...],
            preferred_element_type=F32,
        )
        for r in range(2 * SHARE // LANES):
            at = slice((r % 2) * LANES, (r % 2 + 1) * LANES)
            side = r // 2
            where = found[side : side + 1, at] * COLS + found[2 + side : 3 + side, at]
            slot_node[r] = jnp.broadcast_to(where.astype(jnp.int32), (8, LANES))

    def place(k):
        for p in range(n_dom):
            got = samp_recv[k, p]
            top, rest = split(got)
            values = jnp.concatenate([rest, top, jnp.ones((2, LANES), F32)], axis=0)
            spread(recv_node[p : p + 1] >> 8, values, lhs.at[:, pl.ds(p * LANES, LANES)])
        placed = by_node(
            jnp.dot(lhs[:, pl.ds(0, n_arr)], oh_recv_t[...], preferred_element_type=F32)
        )
        old, row = node[...], sub(node.shape)
        both = placed + pltpu.roll(placed, 3, 0)
        new = jnp.where((row >= 3) & (row < 6), old + DT * both, old)
        if k == 0:
            flag = flag_in[...].astype(F32)
            share = jnp.where(row == 7, flag, 1.0 - flag)
            new = jnp.where(row >= 6, placed * share, new)
        node[...] = new

    def element_cols(k):
        top, rest = split(by_run(node[...]))
        table = jnp.concatenate([top, rest], axis=0).astype(BF16)
        first = sub((8, COLS)) < 3
        for i in range(n_el // COLS):
            at = pl.ds(i * COLS, COLS)
            for pair in range(4):
                with_inner, with_outer = [], []
                for j in (2 * pair, 2 * pair + 1):
                    found = jnp.dot(table, oh_elem[j, :, at], preferred_element_type=F32)
                    high = high_rows[j, :, at]
                    got = jnp.zeros((8, COLS), F32)
                    for h in range(runs):
                        both = found[8 * h : 8 * h + 8] + found[8 * (runs + h) : 8 * (runs + h) + 8]
                        got = jnp.where(high == h, both, got)
                    if k == 0:
                        inn[j, :, at] = jnp.broadcast_to(got[6:7], got.shape)
                        out[j, :, at] = jnp.broadcast_to(got[7:8], got.shape)
                    with_inner.append(jnp.where(first, got, got * inn[j, :, at]))
                    with_outer.append(got * out[j, :, at])
                blocks = split(jnp.concatenate(with_inner, axis=0))
                blocks += split(jnp.concatenate(with_outer, axis=0))
                blocks += (blocks[0], blocks[2])
                for which, block in enumerate(blocks):
                    cols[pl.ds(64 * which + 16 * pair, 16), at] = block.astype(BF16)

    def element_response():
        wide = n_el // 2
        first = sub((8, wide)) < 3
        for i in range(2):
            at = pl.ds(i * wide, wide)
            response = jnp.dot(kblock[...], cols[:, at], preferred_element_type=F32)
            mod = jnp.broadcast_to(modulus[:, at], (8, wide))
            for j in range(8):
                value = mod * (
                    response[8 * j : 8 * j + 8]
                    + out[j, :, at] * response[64 + 8 * j : 72 + 8 * j]
                    + inn[j, :, at] * response[128 + 8 * j : 136 + 8 * j]
                )
                top, rest = split(value)
                spread(elem[j : j + 1, at] >> 8, jnp.where(first, top, rest), lhs.at[:, pl.ds(j * n_el + i * wide, wide)])

    def element_add():
        total = jnp.dot(lhs[...], oh_elem_t[...], preferred_element_type=F32)
        both = by_node(total)
        force[...] = both + pltpu.roll(both, 5, 0)

    def rim_copy(k, side):
        there = lax.rem(me_d + (n_dom - 1 if side == 0 else 1), n_dom)
        return pltpu.make_async_remote_copy(
            src_ref=rim_send.at[k, side],
            dst_ref=rim_recv.at[k, 1 - side],
            send_sem=r_send_sem.at[k, side],
            recv_sem=r_recv_sem.at[k, 1 - side],
            device_id=(me_s, there),
            device_id_type=MESH,
        )

    def rim_start(k):
        for side in range(2):
            for half in range(SHARE // LANES):
                index = slot_node[2 * side + half]
                low, high = index & (LANES - 1), index >> 7
                got = jnp.zeros((8, LANES), F32)
                for r in range(n_nodes // LANES):
                    piece = take_lanes(force[:, pl.ds(r * LANES, LANES)], low)
                    got = jnp.where(high == r, piece, got)
                rim_send[k, side, :, pl.ds(half * LANES, LANES)] = got[:3]
            rim_copy(k, side).start()

    def rim_finish(k):
        for side in range(2):
            rim_copy(k, side).wait_send()
            rim_copy(k, 1 - side).wait_recv()
        tables = []
        for r in range(2 * SHARE // LANES):
            got = rim_recv[k, r // 2, :, pl.ds((r % 2) * LANES, LANES)]
            tables.append(jnp.concatenate([got, jnp.zeros((5, LANES), F32)], axis=0))
        for i in range(n_nodes // LANES):
            at = pl.ds(i * LANES, LANES)
            index = jnp.broadcast_to(slot_in[:, at], (8, LANES))
            low, high = index & (LANES - 1), index >> 7
            extra = jnp.zeros((8, LANES), F32)
            for r, piece in enumerate(tables):
                extra = jnp.where(high == r, take_lanes(piece, low), extra)
            u = node[:, at]
            following = (2.0 * u - prev[:, at]) + DT_SITE2 * (force[:, at] + extra) / mass_in[:, at]
            prev[:, at] = u
            node[:, at] = jnp.where(sub(u.shape) < 3, following, u)

    for x in range(cx):
        y_pack(0, STRESS_Y, x, {f: st[f, x + 2] for f, _ in STRESS_Y})
    expected = (
        n_dom - 1 + jnp.where(me_s > 0, 1, 0) + jnp.where(me_s < n_site - 1, 1, 0)
    ).astype(jnp.int32)
    pl.semaphore_wait(barrier, expected)
    halo_start(0, STRESS_X, STRESS_Y)
    prep_cell()
    prep_nodes()
    prep_k()
    prep_arr()
    prep_slot()
    for k in range(STEPS):
        halo_wait(0, STRESS_X, STRESS_Y)
        velocity_half()
        halo_start(1, VEL_X, VEL_Y)
        sample(k)
        sample_start(k)
        if k == 0:
            prep_hot()
        else:
            element_response()
            element_add()
            rim_start(k - 1)
        halo_wait(1, VEL_X, VEL_Y)
        stress_half()
        if k < STEPS - 1:
            halo_start(0, STRESS_X, STRESS_Y)
        else:
            store = pltpu.make_async_copy(st.at[:, pl.ds(2, cx)], basin_out, out_sem)
            store.start()
        sample_wait(k)
        if k:
            rim_finish(k - 1)
        place(k)
        element_cols(k)
    element_response()
    element_add()
    rim_start(STEPS - 1)
    rim_finish(STEPS - 1)
    for c in range(3):
        disp_v[c] = node[c : c + 1, :]
    disp_store = pltpu.make_async_copy(disp_v, disp_out, in_sem)
    disp_store.start()
    disp_store.wait()
    store.wait()


def hand_over(basin_in, disp_in, basin_out, disp_out, basin, disp, load_sems, store_sems):
    loads = [pltpu.make_async_copy(basin_in.at[f], basin.at[f], load_sems.at[f]) for f in range(9)]
    loads.append(pltpu.make_async_copy(disp_in, disp, load_sems.at[9]))
    stores = [
        pltpu.make_async_copy(basin.at[f], basin_out.at[f], store_sems.at[f]) for f in range(9)
    ]
    stores.append(pltpu.make_async_copy(disp, disp_out, store_sems.at[9]))
    for copy in loads:
        copy.start()
    for load, store in zip(loads, stores):
        load.wait()
        store.start()
    for copy in stores:
        copy.wait()


def solution(mesh):
    n_site, n_dom = mesh.shape["site"], mesh.shape["dom"]

    def on_device(
        fields, material, send_cell, recv_node, elements, modulus, node_mass, outer_flag, shared_slot, stiffness,
        disp_now, disp_prev,
    ):
        _, cx, cy, nz = fields.shape
        n_nodes = disp_now.shape[3]
        n_el = elements.shape[3]
        runs = n_nodes // COLS
        n_arr = n_dom * LANES
        hbm = pl.BlockSpec(memory_space=pltpu.HBM)
        sem = pltpu.SemaphoreType.DMA
        operands = (
            fields, material, send_cell[0, 0], recv_node[0, 0], elements[0, 0], modulus[0], node_mass[0], outer_flag[0],
            shared_slot[0], stiffness, disp_now.reshape(3, 1, n_nodes), disp_prev.reshape(3, 1, n_nodes),
        )
        shapes = (
            jax.ShapeDtypeStruct(fields.shape, F32),
            jax.ShapeDtypeStruct((3, 1, n_nodes), F32),
        )
        basin, disp = pl.pallas_call(
            functools.partial(kernel, n_site, n_dom),
            out_shape=shapes,
            in_specs=[hbm] * 12,
            out_specs=(hbm, hbm),
            scratch_shapes=[
                *(pltpu.VMEM(v.shape, v.dtype) for v in operands[1:]),
                pltpu.VMEM((3, 1, n_nodes), F32),
                pltpu.VMEM((9, cx + 4, cy, nz), F32),
                pltpu.VMEM((2, 6, cx, nz), F32),
                pltpu.VMEM((2, 6, cx, nz), F32),
                pltpu.VMEM((2, 6, cx, nz), F32),
                pltpu.VMEM((2, 6, cx, nz), F32),
                pltpu.VMEM((STEPS, n_dom, 3, LANES), F32),
                pltpu.VMEM((STEPS, n_dom, 3, LANES), F32),
                pltpu.VMEM((STEPS, 2, 3, SHARE), F32),
                pltpu.VMEM((STEPS, 2, 3, SHARE), F32),
                pltpu.VMEM((COLS, n_arr), BF16),
                pltpu.VMEM((n_arr, COLS), BF16),
                pltpu.VMEM((8, COLS, n_el), BF16),
                pltpu.VMEM((8 * n_el, COLS), BF16),
                pltpu.VMEM((COLS, n_nodes), BF16),
                pltpu.VMEM((n_nodes, COLS), BF16),
                pltpu.VMEM((nz, n_arr), BF16),
                pltpu.VMEM((8, 8, n_el), jnp.int32),
                pltpu.VMEM((8 * runs, 8 * n_el), BF16),
                pltpu.VMEM((8, 8, n_el), F32),
                pltpu.VMEM((8, 8, n_el), F32),
                pltpu.VMEM((384, n_el), BF16),
                pltpu.VMEM((192, 384), BF16),
                pltpu.VMEM((8, n_nodes), F32),
                pltpu.VMEM((8, n_nodes), F32),
                pltpu.VMEM((2 * SHARE // LANES, 8, LANES), jnp.int32),
                pltpu.VMEM((8, n_nodes), F32),
                sem,
                sem,
                sem((11,)),
                sem((2, 2, 3)),
                sem((2, 2, 3)),
                sem((2, 2)),
                sem((2, 2)),
                sem((STEPS, n_dom)),
                sem((STEPS, n_dom)),
                sem((STEPS, 2)),
                sem((STEPS, 2)),
            ],
            compiler_params=pltpu.CompilerParams(
                collective_id=0, has_side_effects=True, vmem_limit_bytes=62 * 1024 * 1024
            ),
        )(*operands)
        basin, disp = pl.pallas_call(
            hand_over,
            out_shape=shapes,
            in_specs=[hbm] * 2,
            out_specs=(hbm, hbm),
            scratch_shapes=[
                pltpu.VMEM(fields.shape, F32),
                pltpu.VMEM((3, 1, n_nodes), F32),
                sem((10,)),
                sem((10,)),
            ],
            compiler_params=pltpu.CompilerParams(vmem_limit_bytes=62 * 1024 * 1024),
        )(basin, disp)
        return basin, disp.reshape(disp_now.shape)

    spread3 = P("site", "dom", None)
    spread4 = P("site", "dom", None, None)
    slab = P(None, "dom", "site", None)
    return jax.shard_map(
        on_device,
        mesh=mesh,
        in_specs=(
            slab, slab, spread4, spread4, spread4, spread3, spread3, spread3, spread3, P(), spread4, spread4,
        ),
        out_specs=(slab, spread4),
        check_vma=False,
    )
```

```python
import functools

import jax
import jax.numpy as jnp
from jax import lax
from jax.experimental import pallas as pl
from jax.experimental.pallas import tpu as pltpu
from jax.sharding import PartitionSpec as P

STEPS = 3
SHARE = 256
C_NEAR = 9.0 / 8.0
C_FAR = 1.0 / 24.0
DT = 0.25
DT_SITE2 = 0.15
MESH = pl.DeviceIdType.MESH
LANES = 128
COLS = 256
F32 = jnp.float32
BF16 = jnp.bfloat16

STRESS_X = ((3, "F"), (6, "B"), (7, "B"))
STRESS_Y = ((6, "B"), (4, "F"), (8, "B"))
VEL_X = ((0, "B"), (1, "F"), (2, "F"))
VEL_Y = ((0, "F"), (1, "B"), (2, "F"))
LOW = {"B": 2, "F": 1}
HIGH = {"B": 1, "F": 2}


def take_lanes(table, lanes):
    return lax.gather(
        table,
        lanes[..., None],
        lax.GatherDimensionNumbers(
            offset_dims=(),
            collapsed_slice_dims=(1,),
            start_index_map=(1,),
            operand_batching_dims=(0,),
            start_indices_batching_dims=(0,),
        ),
        (1, 1),
        mode=lax.GatherScatterMode.PROMISE_IN_BOUNDS,
    )


def stencil(kind, m2, m1, f, p1, p2):
    if kind == "B":
        return C_NEAR * (f - m1) - C_FAR * (p1 - m2)
    return C_NEAR * (p1 - f) - C_FAR * (p2 - m1)


def diff_rolled(kind, f, axis, index, low, high):
    n = f.shape[axis]
    below = lambda v, edge: jnp.where(index == 0, edge, pltpu.roll(v, 1, axis))
    above = lambda v, edge: jnp.where(index == n - 1, edge, pltpu.roll(v, n - 1, axis))
    m1 = below(f, low[-1])
    p1 = above(f, high[0])
    if kind == "B":
        return stencil(kind, below(m1, low[0]), m1, f, p1, None)
    return stencil(kind, None, m1, f, p1, above(p1, high[1]))


def split(v):
    top = v.astype(BF16).astype(F32)
    return top, v - top


def kernel(
    n_site,
    n_dom,
    fields,
    mat_hbm,
    send_cell_hbm,
    recv_node_hbm,
    elem_hbm,
    modulus_hbm,
    mass_in_hbm,
    flag_in_hbm,
    slot_in_hbm,
    stiff_hbm,
    now_in_hbm,
    prev_in_hbm,
    basin_out,
    disp_out,
    mat,
    send_cell,
    recv_node,
    elem,
    modulus,
    mass_in,
    flag_in,
    slot_in,
    stiff,
    now_in,
    prev_in,
    disp_v,
    st,
    y_low,
    y_high,
    y_to_low,
    y_to_high,
    samp_send,
    samp_recv,
    rim_send,
    rim_recv,
    oh_recv,
    oh_recv_t,
    oh_elem,
    oh_elem_t,
    oh_slot,
    oh_slot_t,
    oh_cell,
    high_rows,
    lhs,
    inn,
    out,
    cols,
    kblock,
    node,
    prev,
    slot_node,
    force,
    in_sem,
    out_sem,
    in_sems,
    x_send_sem,
    x_recv_sem,
    y_send_sem,
    y_recv_sem,
    s_send_sem,
    s_recv_sem,
    r_send_sem,
    r_recv_sem,
):
    cx, cy, nz = mat.shape[1:]
    n_nodes = node.shape[1]
    runs = n_nodes // COLS
    n_el = elem.shape[1]
    n_arr = n_dom * LANES
    me_s = lax.axis_index("site")
    me_d = lax.axis_index("dom")

    load = pltpu.make_async_copy(fields, st.at[:, pl.ds(2, cx)], in_sem)
    load.start()
    inputs = [
        pltpu.make_async_copy(src, dst, in_sems.at[i])
        for i, (src, dst) in enumerate(
            (
                (mat_hbm, mat),
                (send_cell_hbm, send_cell),
                (recv_node_hbm, recv_node),
                (elem_hbm, elem),
                (modulus_hbm, modulus),
                (mass_in_hbm, mass_in),
                (flag_in_hbm, flag_in),
                (slot_in_hbm, slot_in),
                (stiff_hbm, stiff),
                (now_in_hbm, now_in),
                (prev_in_hbm, prev_in),
            )
        )
    ]
    for copy in inputs:
        copy.start()
    st[:, pl.ds(0, 2)] = jnp.zeros((9, 2, cy, nz), F32)
    st[:, pl.ds(2 + cx, 2)] = jnp.zeros((9, 2, cy, nz), F32)
    y_low[...] = jnp.zeros(y_low.shape, F32)
    y_high[...] = jnp.zeros(y_high.shape, F32)

    barrier = pltpu.get_barrier_semaphore()

    def greet(d, carry):
        pl.semaphore_signal(
            barrier, inc=1, device_id=(me_s, lax.rem(me_d + d, n_dom)), device_id_type=MESH
        )
        return carry

    lax.fori_loop(1, n_dom, greet, 0)
    for step in (-1, 1):
        there = me_s + step

        @pl.when((there >= 0) & (there < n_site))
        def _():
            pl.semaphore_signal(barrier, inc=1, device_id=(there, me_d), device_id_type=MESH)

    load.wait()
    for copy in inputs:
        copy.wait()

    row_iota = lax.broadcasted_iota(jnp.int32, (cy, nz), 0)
    lane_iota = lax.broadcasted_iota(jnp.int32, (cy, nz), 1)

    def x_copies(which, fields_x, upward):
        made = []
        for at, (f, kind) in enumerate(fields_x):
            if upward:
                width = LOW[kind]
                src = st.at[f, pl.ds(2 + cx - width, width)]
                dst = st.at[f, pl.ds(2 - width, width)]
                there = me_d + 1
            else:
                width = HIGH[kind]
                src = st.at[f, pl.ds(2, width)]
                dst = st.at[f, pl.ds(2 + cx, width)]
                there = me_d - 1
            sem = (which, 1 if upward else 0, at)
            made.append(
                pltpu.make_async_remote_copy(
                    src_ref=src,
                    dst_ref=dst,
                    send_sem=x_send_sem.at[sem],
                    recv_sem=x_recv_sem.at[sem],
                    device_id=(me_s, there),
                    device_id_type=MESH,
                )
            )
        return made

    def y_copy(which, fields_y, upward):
        count = sum((LOW if upward else HIGH)[kind] for _, kind in fields_y)
        src, dst = (y_to_high, y_low) if upward else (y_to_low, y_high)
        sem = (which, 1 if upward else 0)
        return pltpu.make_async_remote_copy(
            src_ref=src.at[which, pl.ds(0, count)],
            dst_ref=dst.at[which, pl.ds(0, count)],
            send_sem=y_send_sem.at[sem],
            recv_sem=y_recv_sem.at[sem],
            device_id=(me_s + (1 if upward else -1), me_d),
            device_id_type=MESH,
        )

    has = {
        "x": (me_d > 0, me_d < n_dom - 1),
        "y": (me_s > 0, me_s < n_site - 1),
    }

    def halo_start_x(which, fields_x):
        for upward in (False, True):

            @pl.when(has["x"][upward])
            def _():
                for copy in x_copies(which, fields_x, upward):
                    copy.start()

    def halo_start_y(which, fields_y):
        for upward in (False, True):

            @pl.when(has["y"][upward])
            def _():
                y_copy(which, fields_y, upward).start()

    def halo_wait(which, fields_x, fields_y):
        for upward in (False, True):

            @pl.when(has["x"][upward])
            def _():
                for copy in x_copies(which, fields_x, upward):
                    copy.wait_send()

            @pl.when(has["x"][not upward])
            def _():
                for copy in x_copies(which, fields_x, upward):
                    copy.wait_recv()

            @pl.when(has["y"][upward])
            def _():
                y_copy(which, fields_y, upward).wait_send()

            @pl.when(has["y"][not upward])
            def _():
                y_copy(which, fields_y, upward).wait_recv()

    def y_pack(which, fields_y, x, planes):
        at = 0
        for f, kind in fields_y:
            for k in range(LOW[kind]):
                y = cy - LOW[kind] + k
                y_to_high[which, at, x : x + 1, :] = planes[f][y : y + 1]
                at += 1
        at = 0
        for f, kind in fields_y:
            for k in range(HIGH[kind]):
                y_to_low[which, at, x : x + 1, :] = planes[f][k : k + 1]
                at += 1

    def y_edges(which, fields_y, x):
        edges = {}
        low_at = high_at = 0
        for f, kind in fields_y:
            low = [y_low[which, low_at + k, x : x + 1, :] for k in range(LOW[kind])]
            high = [y_high[which, high_at + k, x : x + 1, :] for k in range(HIGH[kind])]
            low_at += LOW[kind]
            high_at += HIGH[kind]
            edges[f] = (low, high)
        return edges

    def diff_x(kind, f, x):
        at = lambda o: st[f, x + 2 + o]
        if kind == "B":
            return stencil(kind, at(-2), at(-1), at(0), at(1), None)
        return stencil(kind, None, at(-1), at(0), at(1), at(2))

    def diff_y(kind, f, x, edges):
        low, high = edges[f]
        return diff_rolled(kind, st[f, x + 2], 0, row_iota, low, high)

    def diff_z(kind, f, x):
        return diff_rolled(kind, st[f, x + 2], 1, lane_iota, (0.0, 0.0), (0.0, 0.0))

    ends = (0, 1, cx - 2, cx - 1)

    def velocity_half():
        def body(x):
            edges = y_edges(0, STRESS_Y, x)
            b = DT * mat[0, x]
            planes = {
                0: st[0, x + 2]
                + b * (diff_x("F", 3, x) + diff_y("B", 6, x, edges) + diff_z("B", 7, x)),
                1: st[1, x + 2]
                + b * (diff_x("B", 6, x) + diff_y("F", 4, x, edges) + diff_z("B", 8, x)),
                2: st[2, x + 2]
                + b * (diff_x("B", 7, x) + diff_y("B", 8, x, edges) + diff_z("F", 5, x)),
            }
            for f, plane in planes.items():
                st[f, x + 2] = plane
            y_pack(1, VEL_Y, x, planes)

        for x in ends:
            body(x)
        halo_start_x(1, VEL_X)
        for x in range(2, cx - 2):
            body(x)
        halo_start_y(1, VEL_Y)

    def stress_half(last):
        def body(x):
            edges = y_edges(1, VEL_Y, x)
            lam, mu = mat[1, x], mat[2, x]
            exx = diff_x("B", 0, x)
            eyy = diff_y("B", 1, x, edges)
            ezz = diff_z("B", 2, x)
            wide = lam + 2.0 * mu
            shear = DT * mu
            planes = {
                3: st[3, x + 2] + DT * (wide * exx + lam * (eyy + ezz)),
                4: st[4, x + 2] + DT * (wide * eyy + lam * (exx + ezz)),
                5: st[5, x + 2] + DT * (wide * ezz + lam * (exx + eyy)),
                6: st[6, x + 2] + shear * (diff_y("F", 0, x, edges) + diff_x("F", 1, x)),
                7: st[7, x + 2] + shear * (diff_z("F", 0, x) + diff_x("F", 2, x)),
                8: st[8, x + 2] + shear * (diff_z("F", 1, x) + diff_y("F", 2, x, edges)),
            }
            for f, plane in planes.items():
                st[f, x + 2] = plane
            y_pack(0, STRESS_Y, x, planes)

        for x in ends:
            body(x)
        if not last:
            halo_start_x(0, STRESS_X)
        for x in range(2, cx - 2):
            body(x)
        if not last:
            halo_start_y(0, STRESS_Y)

    def sample(k):
        n = n_arr // 2
        for i in range(2):
            cell = [send_cell[q : q + 1] for q in range(i * n_dom // 2, (i + 1) * n_dom // 2)]
            high = jnp.concatenate([jnp.broadcast_to(v >> 8, (8, LANES)) for v in cell], axis=1)
            row = lax.broadcasted_iota(jnp.int32, high.shape, 0)
            for c in range(3):
                parts = split(st[c, pl.ds(2, cx)].reshape(cx * cy, nz))
                table = jnp.concatenate(parts, axis=0).astype(BF16)
                found = jnp.dot(table, oh_cell[:, pl.ds(i * n, n)], preferred_element_type=F32)
                total = jnp.zeros(high.shape, F32)
                for t in range(cx * cy // 8):
                    both = found[8 * t : 8 * t + 8] + found[cx * cy + 8 * t : cx * cy + 8 * t + 8]
                    total = jnp.where(high == row + 8 * t, both, total)
                total = jnp.sum(total, axis=0, keepdims=True)
                for q in range(n_dom // 2):
                    samp_send[k, i * n_dom // 2 + q, c : c + 1, :] = total[
                        :, q * LANES : (q + 1) * LANES
                    ]

    def sample_copy(k, d):
        there = lax.rem(me_d + d, n_dom)
        return pltpu.make_async_remote_copy(
            src_ref=samp_send.at[k, there],
            dst_ref=samp_recv.at[k, me_d],
            send_sem=s_send_sem.at[k, d],
            recv_sem=s_recv_sem.at[k, d],
            device_id=(me_s, there),
            device_id_type=MESH,
        )

    def sample_start(k):
        for d in range(1, n_dom):
            sample_copy(k, d).start()
        samp_recv[k, me_d] = samp_send[k, me_d]

    def sample_wait(k):
        for d in range(1, n_dom):
            here = lax.rem(me_d + n_dom - d, n_dom)
            copy = pltpu.make_async_remote_copy(
                src_ref=samp_send.at[k, here],
                dst_ref=samp_recv.at[k, here],
                send_sem=s_send_sem.at[k, d],
                recv_sem=s_recv_sem.at[k, d],
                device_id=(me_s, here),
                device_id_type=MESH,
            )
            copy.wait_recv()
            sample_copy(k, d).wait_send()

    def run(h):
        return pl.ds(h * COLS, COLS)

    def by_run(value):
        return jnp.concatenate([value[:, h * COLS : (h + 1) * COLS] for h in range(runs)], axis=0)

    def by_node(value):
        return jnp.concatenate([value[8 * h : 8 * h + 8] for h in range(runs)], axis=1)

    def packed(row):
        return jnp.broadcast_to(row.astype(F32), (16, row.shape[1])).astype(BF16)

    def one_hot(low, ref):
        low16 = packed(low)
        iota = lax.broadcasted_iota(jnp.int32, low16.shape, 0).astype(F32).astype(BF16)
        one, zero = jnp.ones(low16.shape, BF16), jnp.zeros(low16.shape, BF16)
        for t in range(COLS // 16):
            ref[pl.ds(16 * t, 16), :] = jnp.where(iota + BF16(16 * t) == low16, one, zero)

    def one_hot_both(low, ref, turned):
        one_hot(low, ref)
        turned[...] = ref[...].T

    def spread(high, values, ref):
        high16 = packed(high)
        twice = jnp.concatenate([values, values], axis=0).astype(BF16)
        second = (lax.broadcasted_iota(jnp.int32, high16.shape, 0) >> 3).astype(F32).astype(BF16)
        zero = jnp.zeros(high16.shape, BF16)
        for t in range(runs // 2):
            ref[pl.ds(16 * t, 16), :] = jnp.where(second + BF16(2 * t) == high16, twice, zero)

    def sub(shape):
        return lax.broadcasted_iota(jnp.int32, shape, 0) & 7

    def prep_nodes():
        node[...] = jnp.zeros(node.shape, F32)
        prev[...] = jnp.zeros(prev.shape, F32)
        for c in range(3):
            node[c : c + 1, :] = now_in[c]
            prev[c : c + 1, :] = prev_in[c]

    def prep_k():
        n_k = stiff.shape[0]
        n_r, n_c = kblock.shape

        def dof(i, comp):
            return comp * 8 + ((i & 63) >> 3)

        def comp3(i):
            r = i & 7
            return jnp.where(r < 3, r, r - 3)

        ri = lax.broadcasted_iota(jnp.int32, (n_r, n_k), 0)
        rk = lax.broadcasted_iota(jnp.int32, (n_r, n_k), 1)
        pick_r = jnp.where((dof(ri, comp3(ri)) == rk) & ((ri & 7) < 6), 1.0, 0.0)
        ck = lax.broadcasted_iota(jnp.int32, (n_k, n_c), 0)
        ci = lax.broadcasted_iota(jnp.int32, (n_k, n_c), 1)
        pick_c = jnp.where((dof(ci, comp3(ci)) == ck) & ((ci & 7) < 6), 1.0, 0.0)
        exact = functools.partial(
            jnp.dot, precision=lax.Precision.HIGHEST, preferred_element_type=F32
        )
        top, rest = split(exact(exact(pick_r, stiff[...]), pick_c))
        group = lax.broadcasted_iota(jnp.int32, (n_r, n_c), 0) >> 6
        ci = lax.broadcasted_iota(jnp.int32, (n_r, n_c), 1)
        block, free_col = ci >> 6, (ci & 7) >= 3
        outer_block = (block == 2) | (block == 3) | (block == 5)
        inner_block = (block == 0) | (block == 1) | (block == 4)
        meant = (
            ((group == 0) & ((ci & 7) < 3) & inner_block)
            | ((group == 1) & free_col & inner_block)
            | ((group == 2) & free_col & outer_block)
        )
        value = jnp.where(block >= 4, rest, top)
        value = jnp.where(group == 1, value, -value)
        kblock[...] = jnp.where(meant, value, 0.0).astype(BF16)

    def prep_arr():
        for p in range(n_dom):
            at = pl.ds(p * LANES, LANES)
            one_hot_both(recv_node[p : p + 1] & (COLS - 1), oh_recv.at[:, at], oh_recv_t.at[at])

    def prep_hot():
        for j in range(8):
            one_hot_both(elem[j : j + 1] & (COLS - 1), oh_elem.at[j], oh_elem_t.at[pl.ds(j * n_el, n_el)])
            high_rows[j] = jnp.broadcast_to(elem[j : j + 1] >> 8, (8, n_el))

    def prep_cell():
        for q in range(n_dom):
            one_hot(send_cell[q : q + 1] & (nz - 1), oh_cell.at[:, pl.ds(q * LANES, LANES)])

    def prep_slot():
        row = slot_in[...]
        one_hot_both(row & (COLS - 1), oh_slot, oh_slot_t)
        ri = lax.broadcasted_iota(jnp.int32, (16, n_nodes), 0)
        li = lax.broadcasted_iota(jnp.int32, (16, n_nodes), 1)
        value = jnp.where(ri < 2, li >> 8, li & (COLS - 1))
        hit = ((row >> 8) == (ri & 1)) & (ri < 4)
        found = jnp.dot(
            jnp.where(hit, value, 0).astype(F32).astype(BF16),
            oh_slot_t[...],
            preferred_element_type=F32,
        )
        for r in range(2 * SHARE // LANES):
            at = slice((r % 2) * LANES, (r % 2 + 1) * LANES)
            side = r // 2
            where = found[side : side + 1, at] * COLS + found[2 + side : 3 + side, at]
            slot_node[r] = jnp.broadcast_to(where.astype(jnp.int32), (8, LANES))

    def place(k):
        for p in range(n_dom):
            got = samp_recv[k, p]
            top, rest = split(got)
            values = jnp.concatenate([rest, top, jnp.ones((2, LANES), F32)], axis=0)
            spread(recv_node[p : p + 1] >> 8, values, lhs.at[:, pl.ds(p * LANES, LANES)])
        placed = by_node(
            jnp.dot(lhs[:, pl.ds(0, n_arr)], oh_recv_t[...], preferred_element_type=F32)
        )
        old, row = node[...], sub(node.shape)
        both = placed + pltpu.roll(placed, 3, 0)
        new = jnp.where((row >= 3) & (row < 6), old + DT * both, old)
        if k == 0:
            flag = flag_in[...].astype(F32)
            share = jnp.where(row == 7, flag, 1.0 - flag)
            new = jnp.where(row >= 6, placed * share, new)
        node[...] = new

    def element_cols(k):
        top, rest = split(by_run(node[...]))
        table = jnp.concatenate([top, rest], axis=0).astype(BF16)
        first = sub((8, COLS)) < 3
        for i in range(n_el // COLS):
            at = pl.ds(i * COLS, COLS)
            for pair in range(4):
                with_inner, with_outer = [], []
                for j in (2 * pair, 2 * pair + 1):
                    found = jnp.dot(table, oh_elem[j, :, at], preferred_element_type=F32)
                    high = high_rows[j, :, at]
                    got = jnp.zeros((8, COLS), F32)
                    for h in range(runs):
                        both = found[8 * h : 8 * h + 8] + found[8 * (runs + h) : 8 * (runs + h) + 8]
                        got = jnp.where(high == h, both, got)
                    if k == 0:
                        inn[j, :, at] = jnp.broadcast_to(got[6:7], got.shape)
                        out[j, :, at] = jnp.broadcast_to(got[7:8], got.shape)
                    with_inner.append(jnp.where(first, got, got * inn[j, :, at]))
                    with_outer.append(got * out[j, :, at])
                blocks = split(jnp.concatenate(with_inner, axis=0))
                blocks += split(jnp.concatenate(with_outer, axis=0))
                blocks += (blocks[0], blocks[2])
                for which, block in enumerate(blocks):
                    cols[pl.ds(64 * which + 16 * pair, 16), at] = block.astype(BF16)

    def element_response():
        wide = n_el // 2
        first = sub((8, wide)) < 3
        for i in range(2):
            at = pl.ds(i * wide, wide)
            response = jnp.dot(kblock[...], cols[:, at], preferred_element_type=F32)
            mod = jnp.broadcast_to(modulus[:, at], (8, wide))
            for j in range(8):
                value = mod * (
                    response[8 * j : 8 * j + 8]
                    + out[j, :, at] * response[64 + 8 * j : 72 + 8 * j]
                    + inn[j, :, at] * response[128 + 8 * j : 136 + 8 * j]
                )
                top, rest = split(value)
                spread(elem[j : j + 1, at] >> 8, jnp.where(first, top, rest), lhs.at[:, pl.ds(j * n_el + i * wide, wide)])

    def element_add():
        total = jnp.dot(lhs[...], oh_elem_t[...], preferred_element_type=F32)
        both = by_node(total)
        force[...] = both + pltpu.roll(both, 5, 0)

    def rim_copy(k, side):
        there = lax.rem(me_d + (n_dom - 1 if side == 0 else 1), n_dom)
        return pltpu.make_async_remote_copy(
            src_ref=rim_send.at[k, side],
            dst_ref=rim_recv.at[k, 1 - side],
            send_sem=r_send_sem.at[k, side],
            recv_sem=r_recv_sem.at[k, 1 - side],
            device_id=(me_s, there),
            device_id_type=MESH,
        )

    def rim_start(k):
        for side in range(2):
            for half in range(SHARE // LANES):
                index = slot_node[2 * side + half]
                low, high = index & (LANES - 1), index >> 7
                got = jnp.zeros((8, LANES), F32)
                for r in range(n_nodes // LANES):
                    piece = take_lanes(force[:, pl.ds(r * LANES, LANES)], low)
                    got = jnp.where(high == r, piece, got)
                rim_send[k, side, :, pl.ds(half * LANES, LANES)] = got[:3]
            rim_copy(k, side).start()

    def rim_finish(k):
        for side in range(2):
            rim_copy(k, side).wait_send()
            rim_copy(k, 1 - side).wait_recv()
        tables = []
        for r in range(2 * SHARE // LANES):
            got = rim_recv[k, r // 2, :, pl.ds((r % 2) * LANES, LANES)]
            tables.append(jnp.concatenate([got, jnp.zeros((5, LANES), F32)], axis=0))
        for i in range(n_nodes // LANES):
            at = pl.ds(i * LANES, LANES)
            index = jnp.broadcast_to(slot_in[:, at], (8, LANES))
            low, high = index & (LANES - 1), index >> 7
            extra = jnp.zeros((8, LANES), F32)
            for r, piece in enumerate(tables):
                extra = jnp.where(high == r, take_lanes(piece, low), extra)
            u = node[:, at]
            following = (2.0 * u - prev[:, at]) + DT_SITE2 * (force[:, at] + extra) / mass_in[:, at]
            prev[:, at] = u
            node[:, at] = jnp.where(sub(u.shape) < 3, following, u)

    for x in range(cx):
        y_pack(0, STRESS_Y, x, {f: st[f, x + 2] for f, _ in STRESS_Y})
    expected = (
        n_dom - 1 + jnp.where(me_s > 0, 1, 0) + jnp.where(me_s < n_site - 1, 1, 0)
    ).astype(jnp.int32)
    pl.semaphore_wait(barrier, expected)
    halo_start_x(0, STRESS_X)
    halo_start_y(0, STRESS_Y)
    prep_cell()
    prep_nodes()
    prep_k()
    prep_arr()
    prep_slot()
    for k in range(STEPS):
        halo_wait(0, STRESS_X, STRESS_Y)
        velocity_half()
        sample(k)
        sample_start(k)
        if k == 0:
            prep_hot()
        else:
            element_response()
            element_add()
            rim_start(k - 1)
        halo_wait(1, VEL_X, VEL_Y)
        stress_half(k == STEPS - 1)
        if k == STEPS - 1:
            store = pltpu.make_async_copy(st.at[:, pl.ds(2, cx)], basin_out, out_sem)
            store.start()
        sample_wait(k)
        if k:
            rim_finish(k - 1)
        place(k)
        element_cols(k)
    element_response()
    element_add()
    rim_start(STEPS - 1)
    rim_finish(STEPS - 1)
    for c in range(3):
        disp_v[c] = node[c : c + 1, :]
    disp_store = pltpu.make_async_copy(disp_v, disp_out, in_sem)
    disp_store.start()
    disp_store.wait()
    store.wait()


def hand_over(basin_in, disp_in, basin_out, disp_out, basin, disp, load_sems, store_sems):
    loads = [pltpu.make_async_copy(basin_in.at[f], basin.at[f], load_sems.at[f]) for f in range(9)]
    loads.append(pltpu.make_async_copy(disp_in, disp, load_sems.at[9]))
    stores = [
        pltpu.make_async_copy(basin.at[f], basin_out.at[f], store_sems.at[f]) for f in range(9)
    ]
    stores.append(pltpu.make_async_copy(disp, disp_out, store_sems.at[9]))
    for copy in loads:
        copy.start()
    for load, store in zip(loads, stores):
        load.wait()
        store.start()
    for copy in stores:
        copy.wait()


def solution(mesh):
    n_site, n_dom = mesh.shape["site"], mesh.shape["dom"]

    def on_device(
        fields, material, send_cell, recv_node, elements, modulus, node_mass, outer_flag, shared_slot, stiffness,
        disp_now, disp_prev,
    ):
        _, cx, cy, nz = fields.shape
        n_nodes = disp_now.shape[3]
        n_el = elements.shape[3]
        runs = n_nodes // COLS
        n_arr = n_dom * LANES
        hbm = pl.BlockSpec(memory_space=pltpu.HBM)
        sem = pltpu.SemaphoreType.DMA
        operands = (
            fields, material, send_cell[0, 0], recv_node[0, 0], elements[0, 0], modulus[0], node_mass[0], outer_flag[0],
            shared_slot[0], stiffness, disp_now.reshape(3, 1, n_nodes), disp_prev.reshape(3, 1, n_nodes),
        )
        shapes = (
            jax.ShapeDtypeStruct(fields.shape, F32),
            jax.ShapeDtypeStruct((3, 1, n_nodes), F32),
        )
        basin, disp = pl.pallas_call(
            functools.partial(kernel, n_site, n_dom),
            out_shape=shapes,
            in_specs=[hbm] * 12,
            out_specs=(hbm, hbm),
            scratch_shapes=[
                *(pltpu.VMEM(v.shape, v.dtype) for v in operands[1:]),
                pltpu.VMEM((3, 1, n_nodes), F32),
                pltpu.VMEM((9, cx + 4, cy, nz), F32),
                pltpu.VMEM((2, 6, cx, nz), F32),
                pltpu.VMEM((2, 6, cx, nz), F32),
                pltpu.VMEM((2, 6, cx, nz), F32),
                pltpu.VMEM((2, 6, cx, nz), F32),
                pltpu.VMEM((STEPS, n_dom, 3, LANES), F32),
                pltpu.VMEM((STEPS, n_dom, 3, LANES), F32),
                pltpu.VMEM((STEPS, 2, 3, SHARE), F32),
                pltpu.VMEM((STEPS, 2, 3, SHARE), F32),
                pltpu.VMEM((COLS, n_arr), BF16),
                pltpu.VMEM((n_arr, COLS), BF16),
                pltpu.VMEM((8, COLS, n_el), BF16),
                pltpu.VMEM((8 * n_el, COLS), BF16),
                pltpu.VMEM((COLS, n_nodes), BF16),
                pltpu.VMEM((n_nodes, COLS), BF16),
                pltpu.VMEM((nz, n_arr), BF16),
                pltpu.VMEM((8, 8, n_el), jnp.int32),
                pltpu.VMEM((8 * runs, 8 * n_el), BF16),
                pltpu.VMEM((8, 8, n_el), F32),
                pltpu.VMEM((8, 8, n_el), F32),
                pltpu.VMEM((384, n_el), BF16),
                pltpu.VMEM((192, 384), BF16),
                pltpu.VMEM((8, n_nodes), F32),
                pltpu.VMEM((8, n_nodes), F32),
                pltpu.VMEM((2 * SHARE // LANES, 8, LANES), jnp.int32),
                pltpu.VMEM((8, n_nodes), F32),
                sem,
                sem,
                sem((11,)),
                sem((2, 2, 3)),
                sem((2, 2, 3)),
                sem((2, 2)),
                sem((2, 2)),
                sem((STEPS, n_dom)),
                sem((STEPS, n_dom)),
                sem((STEPS, 2)),
                sem((STEPS, 2)),
            ],
            compiler_params=pltpu.CompilerParams(
                collective_id=0, has_side_effects=True, vmem_limit_bytes=62 * 1024 * 1024
            ),
        )(*operands)
        basin, disp = pl.pallas_call(
            hand_over,
            out_shape=shapes,
            in_specs=[hbm] * 2,
            out_specs=(hbm, hbm),
            scratch_shapes=[
                pltpu.VMEM(fields.shape, F32),
                pltpu.VMEM((3, 1, n_nodes), F32),
                sem((10,)),
                sem((10,)),
            ],
            compiler_params=pltpu.CompilerParams(vmem_limit_bytes=62 * 1024 * 1024),
        )(basin, disp)
        return basin, disp.reshape(disp_now.shape)

    spread3 = P("site", "dom", None)
    spread4 = P("site", "dom", None, None)
    slab = P(None, "dom", "site", None)
    return jax.shard_map(
        on_device,
        mesh=mesh,
        in_specs=(
            slab, slab, spread4, spread4, spread4, spread3, spread3, spread3, spread3, P(), spread4, spread4,
        ),
        out_specs=(slab, spread4),
        check_vma=False,
    )
```
